32 devices in a mesh: section: 2 (over core), dp: 4 (over z), tensor: 4 (over y, x).
Axes of the slice: x: 2, y: 2, z: 4, core: 2. Of those that a mesh axis runs over, the one named last changes fastest.
Arguments:
- inputs: bfloat16 [2, 4096, 1536], P(None, ('dp', 'tensor')), may hold values from -6 to 6
- cotangent: float32 [2, 4096, 1536], P(None, ('dp', 'tensor')), may hold values from -6 to 6
- segments: int32 [2, 4, 1024], P(None, 'dp'), may hold values from 0 to 3, never falling along the last dimension, each value on 1 to 896 neighbouring positions
- routes: int32 [2, 2, 4096, 4], P('section', None, ('dp', 'tensor')), may hold values from 0 to 7, all different within a row; in each aligned block of 256 rows (0 to 255, 256 to 511, ..., all dimensions but the last counted through in order) at most 145 rows name the same one
- route_gates: float32 [2, 2, 4096, 4], P('section', None, ('dp', 'tensor')), may hold values from 0.1 to 0.4
- attn_gain: float32 [2, 1536], P('section'), may hold values from 0.5 to 1.5
- w_query: bfloat16 [2, 1536, 1536], P('section', None, 'tensor'), may hold values from -0.15625 to 0.15625
- key_weight: bfloat16 [2, 1536, 256], P('section'), may hold values from -0.15625 to 0.15625
- value_weight: bfloat16 [2, 1536, 256], P('section'), may hold values from -0.15625 to 0.15625
- w_out: bfloat16 [2, 1536, 1536], P('section', 'tensor'), may hold values from -0.625 to 0.625
- mixer_gain: float32 [2, 1536], P('section'), may hold values from 0.5 to 1.5
- w_gate: bfloat16 [2, 8, 1536, 768], P('section', 'dp', None, 'tensor'), may hold values from -0.15625 to 0.15625
- w_up: bfloat16 [2, 8, 1536, 768], P('section', 'dp', None, 'tensor'), may hold values from -0.15625 to 0.15625
- w_down: bfloat16 [2, 8, 768, 1536], P('section', 'dp', 'tensor'), may hold values from -0.4375 to 0.4375
Outputs:
- layer_outputs: bfloat16 [2, 2, 4096, 1536], P('section', None, ('dp', 'tensor'))
- input_grads: float32 [2, 2, 4096, 1536], P('section', None, ('dp', 'tensor'))
- grad_attn_gain: float32 [2, 1536], P('section')
- grad_w_query: float32 [2, 1536, 1536], P('section', None, 'tensor')
- grad_w_key: float32 [2, 1536, 256], P('section')
- grad_w_value: float32 [2, 1536, 256], P('section')
- grad_w_out: float32 [2, 1536, 1536], P('section', 'tensor')
- grad_mixer_gain: float32 [2, 1536], P('section')
- grad_w_gate: float32 [2, 8, 1536, 768], P('section', 'dp', None, 'tensor')
- grad_w_up: float32 [2, 8, 1536, 768], P('section', 'dp', None, 'tensor')
- grad_w_down: float32 [2, 8, 768, 1536], P('section', 'dp', 'tensor')
The draws below stay inside these ranges and needn't reach their ends.
Inputs may be any that keep to these rules, and one draw needn't show every extreme that they name: `routes`: each row names 4 different experts. In every aligned block of 256 rows (one device's rows of one layer and micro-batch) no expert is named more than 145 times, and in some blocks one is named exactly 145 times. `segments`: along each sequence the numbers start at 0, never fall and rise by one at each new document; each sequence has 4 documents, the longest of exactly 896 tokens.
All inputs are finite; a program needn't handle non-finite values.
Results may differ from the reference program's by a relative error of at most 0.03.
Values may be sent and summed in bfloat16 or wider, within the bound.
A program may use at most 384 MiB of HBM per device.

```python
import math
import jax
import jax.numpy as jnp
import numpy as np
from jax import lax

MODEL_DIM = 1536
QUERY_HEADS = 12
KEY_VALUE_HEADS = 2
HEAD_DIM = 128
FFE = 768
TOP = 4
EXP_DEV = 2
SEQUENCE_TOKENS = 1024
MB = 2
EXPERTS = 8
SEQS = 4
R = 256
CAPQ = 145
N_SECTION = 2
N_DP = 4


def steps_of(key, dims, split, smallest, high):
    loudness, own = 1.0, jax.random.fold_in(key, 6)
    for position, shards_of in split:
        heights = jnp.exp(jax.random.uniform(jax.random.fold_in(own, position), (shards_of,), jnp.float32, smallest / len(split), high / len(split)))
        loudness = loudness * jnp.repeat(heights, dims[position] // shards_of).reshape([-1 if axis == position else 1 for axis in range(len(dims))])
    return loudness


def profile(count, total, bound, skew):
    weights = [(1 << 20) // math.isqrt(rank ** skew) + 1 for rank in range(2, count + 1)]
    surplus, holding = total - bound - (count - 1), [1] * (count - 1)
    while surplus > 0:
        candidates = [i for i in range(count - 1) if holding[i] < bound]
        mass, budget = sum([weights[i] for i in candidates]), surplus
        for i in candidates:
            extra = min(bound - holding[i], max(1, budget * weights[i] // mass), surplus)
            holding[i] = holding[i] + extra
            surplus = surplus - extra
    return np.array([bound] + holding)


def uneven_parts(rng, amount, total, bound, lean):
    if amount == 2:
        one = jax.random.randint(rng, (), max(1, total - bound), min(bound, total - 1) + 1)
        return jnp.stack([one, total - one])
    sizes = jnp.asarray(profile(amount, total, bound, lean), jnp.int32)
    pairs = (amount - 1) // 2
    donor, taker = sizes[1:1 + 2 * pairs:2], sizes[2:2 + 2 * pairs:2]
    room = jnp.minimum(donor - 1, bound - taker)
    passed = jax.random.randint(jax.random.fold_in(rng, 1), (pairs,), 0, 1 << 20) % (room + 1)
    sizes = sizes.at[1:1 + 2 * pairs:2].set(donor - passed).at[2:2 + 2 * pairs:2].set(taker + passed)
    return sizes[jax.random.permutation(jax.random.fold_in(rng, 2), amount)]


def routed_block(own_key, own, number, rows, number_of, top, most, slope):
    order = jax.random.permutation(own_key, number_of)
    crowded, usual = portions_of(number_of, rows * top, most, slope, True), portions_of(number_of, rows * top, most, slope, False)
    places = jnp.arange(number_of)

    def named(tallies, offset_by):
        used = int((tallies > 0).sum())
        fixed = max(1, used // 4)
        passed = fixed + (places - fixed + offset_by * (used - fixed)) % max(1, number_of - fixed)
        return jnp.zeros((number_of,), jnp.int32).at[order[jnp.where(places < fixed, places, passed)]].set(jnp.asarray(tallies, jnp.int32))

    tallies = jnp.where(number % 4 == 0, named(crowded, number // 4), named(usual, number - number // 4 - 1))
    mixed = jax.random.permutation(jax.random.fold_in(own, 3), number_of)
    giver, taker = mixed[0:number_of // 2 * 2:2], mixed[1:number_of // 2 * 2:2]
    margin = jnp.minimum(tallies[giver] - 1, most - tallies[taker]) // 2
    margin = jnp.where((giver == order[0]) | (taker == order[0]) | (tallies[taker] == 0), 0, jnp.maximum(margin, 0))
    passed = jax.random.randint(jax.random.fold_in(own, 4), (number_of // 2,), 0, 1 << 20) % (margin + 1)
    tallies = tallies.at[giver].add(-passed).at[taker].add(passed)
    members = jnp.searchsorted(jnp.cumsum(tallies), jnp.arange(rows * top), side="right").astype(jnp.int32)
    grid = members.reshape(top, rows).T
    grid = grid[jax.random.permutation(jax.random.fold_in(own, 1), rows)]
    offset_by = jax.random.randint(jax.random.fold_in(own, 2), (rows, 1), 0, top)
    return jnp.take_along_axis(grid, (jnp.arange(top)[None, :] + offset_by) % top, axis=1)


def portions_of(amount, total, reach, slope, full):
    portions = [(1 << 20) // math.isqrt(rank ** slope) + 1 for rank in range(1, amount + 1)]
    largest = reach if full else min(reach, max(-(-total // amount), total * portions[0] // sum(portions)))
    least = 1 if total - largest >= amount - 1 else 0
    holding, spare = [largest] + [least] * (amount - 1), total - largest - least * (amount - 1)
    while spare > 0:
        free = [i for i in range(1, amount) if holding[i] < largest] or [i for i in range(1, amount) if holding[i] < reach]
        pool, remaining = sum([portions[i] for i in free]), spare
        for i in free:
            addition = min(reach - holding[i], max(1, remaining * portions[i] // pool), spare)
            holding[i] = holding[i] + addition
            spare = spare - addition
    return np.array(holding)


def normal_values(rng, extent, scale, most, cuts=(), held_as=jnp.bfloat16):
    factor_of = steps_of(rng, extent, cuts, -0.22, 0.18) if cuts else 1.0
    result = jax.random.normal(rng, extent, jnp.float32) * scale * factor_of
    return jnp.minimum(jnp.maximum(result, -most), most).astype(held_as)


def setup_inputs(seed: int = 0) -> dict:
    keys = jax.random.split(jax.random.key(seed), 15)
    inputs = normal_values(keys[0], (MB, SEQS * SEQUENCE_TOKENS, MODEL_DIM), 1.0, 6.0, ((1, 16),))
    cotangent = normal_values(keys[1], (MB, SEQS * SEQUENCE_TOKENS, MODEL_DIM), 1.0, 6.0, ((1, 16),), jnp.float32)
    segments = jax.vmap(lambda own: jnp.searchsorted(jnp.cumsum(uneven_parts(own, 4, SEQUENCE_TOKENS, SEQUENCE_TOKENS * 7 // 8, 1)), jnp.arange(SEQUENCE_TOKENS), side="right"))(jax.random.split(keys[2], MB * SEQS)).reshape((MB, SEQS, SEQUENCE_TOKENS)).astype(jnp.int32)
    routes_keys = jax.random.split(jax.random.fold_in(keys[3], 1), N_SECTION * MB * (SEQS * SEQUENCE_TOKENS) // R)
    routes_turns = jax.random.permutation(jax.random.fold_in(keys[3], 3), N_SECTION * MB * (SEQS * SEQUENCE_TOKENS) // R)
    routes = jax.vmap(lambda own, number: routed_block(jax.random.fold_in(keys[3], 2), own, number, R, EXP_DEV * N_DP, TOP, CAPQ, 0))(routes_keys, routes_turns).reshape((N_SECTION, MB, SEQS * SEQUENCE_TOKENS, TOP))
    route_gates = jnp.clip(0.1 + 0.3 * jax.random.uniform(keys[4], (N_SECTION, MB, SEQS * SEQUENCE_TOKENS, TOP), jnp.float32) ** steps_of(keys[4], (N_SECTION, MB, SEQS * SEQUENCE_TOKENS, TOP), ((0, 2), (2, 16)), -0.2, 0.2), 0.1, 0.4)
    attn_gain = jnp.clip(1.0 + 0.1 * jax.random.normal(keys[5], (N_SECTION, MODEL_DIM), jnp.float32), 0.5, 1.5)
    w_query = normal_values(keys[6], (N_SECTION, MODEL_DIM, QUERY_HEADS * HEAD_DIM), MODEL_DIM ** -0.5, 0.15625, ((0, 2), (2, 4)))
    key_weight = normal_values(keys[7], (N_SECTION, MODEL_DIM, KEY_VALUE_HEADS * HEAD_DIM), MODEL_DIM ** -0.5, 0.15625, ((0, 2),))
    value_weight = normal_values(keys[8], (N_SECTION, MODEL_DIM, KEY_VALUE_HEADS * HEAD_DIM), MODEL_DIM ** -0.5, 0.15625, ((0, 2),))
    w_out = normal_values(keys[9], (N_SECTION, QUERY_HEADS * HEAD_DIM, MODEL_DIM), (QUERY_HEADS * HEAD_DIM // 16) ** -0.5, 0.625, ((0, 2), (1, 4)))
    mixer_gain = jnp.clip(1.0 + 0.1 * jax.random.normal(keys[10], (N_SECTION, MODEL_DIM), jnp.float32), 0.5, 1.5)
    w_gate = normal_values(keys[11], (N_SECTION, EXPERTS, MODEL_DIM, FFE), MODEL_DIM ** -0.5, 0.15625, ((0, 2), (1, 4), (3, 4)))
    w_up = normal_values(keys[12], (N_SECTION, EXPERTS, MODEL_DIM, FFE), MODEL_DIM ** -0.5, 0.15625, ((0, 2), (1, 4), (3, 4)))
    w_down = normal_values(keys[13], (N_SECTION, EXPERTS, FFE, MODEL_DIM), (FFE // 4) ** -0.5, 0.4375, ((0, 2), (1, 4), (2, 4)))
    return dict(inputs=inputs, cotangent=cotangent, segments=segments, routes=routes, route_gates=route_gates, attn_gain=attn_gain, w_query=w_query, key_weight=key_weight, value_weight=value_weight, w_out=w_out, mixer_gain=mixer_gain, w_gate=w_gate, w_up=w_up, w_down=w_down)


HIGHEST = lax.Precision.HIGHEST
EPSILON = 1e-06

@jax.custom_vjp
def low(v):
    return lax.optimization_barrier(v.astype(jnp.bfloat16)).astype(jnp.float32)

@jax.custom_vjp
def low_back(v):
    return v

def low_keep(v):
    return (low(v), None)

def low_pass(kept, grad):
    return (grad,)

def back_keep(v):
    return (v, None)

def back_low(kept, grad):
    return (low(grad),)
low.defvjp(low_keep, low_pass)
low_back.defvjp(back_keep, back_low)

def rms_norm(values, gain_vec):
    return values * lax.rsqrt(lax.optimization_barrier(jnp.mean(values * values, axis=-1, keepdims=True)) + EPSILON) * gain_vec

def rotary_apply(values):
    length = values.shape[-3]
    head_size = values.shape[-1]
    half_size = head_size // 2
    places = jnp.arange(length, dtype=jnp.float32)
    freq_rates = 10000.0 ** (-jnp.arange(half_size, dtype=jnp.float32) * 2.0 / head_size)
    angles = places[:, None] * freq_rates[None, :]
    cosine = jnp.cos(angles)[:, None, :]
    sine_part = jnp.sin(angles)[:, None, :]
    leading = values[..., :half_size]
    second = values[..., half_size:]
    return jnp.concatenate([leading * cosine - second * sine_part, second * cosine + leading * sine_part], axis=-1)

def attend_one(packed):
    queries, key_token_rows, value_token_rows, segment = packed
    length = queries.shape[0]
    group_factor = QUERY_HEADS // KEY_VALUE_HEADS
    key_wide = jnp.repeat(key_token_rows, group_factor, axis=1)
    value_wide = jnp.repeat(value_token_rows, group_factor, axis=1)
    scores = jnp.einsum('qhd,khd->hqk', queries, key_wide, precision=HIGHEST) * HEAD_DIM ** (-0.5)
    scores = low_back(scores)
    places = jnp.arange(length)
    allowed = (places[None, :] <= places[:, None]) & (segment[:, None] == segment[None, :])
    scores = jnp.where(allowed[None], scores, -1e+30)
    attn_probs = low(jax.nn.softmax(scores, axis=-1))
    mixture = jnp.einsum('hqk,khd->qhd', attn_probs, value_wide, precision=HIGHEST)
    return mixture.reshape(length, -1)

def layer_apply(values_in, segment_rows, route_now, gate_now, attn_gain, w_query, key_weight, value_weight, w_out, mixer_gain, w_gate, w_up, w_down):
    token_count = values_in.shape[0]
    sequence_count = token_count // SEQUENCE_TOKENS
    normed = low(rms_norm(values_in, attn_gain))
    query_lin = low_back(jnp.dot(normed, w_query, precision=HIGHEST))
    queries = low(rotary_apply(query_lin.reshape(sequence_count, SEQUENCE_TOKENS, QUERY_HEADS, HEAD_DIM)))
    key_linear = low_back(jnp.dot(normed, key_weight, precision=HIGHEST))
    key_token_rows = low(rotary_apply(key_linear.reshape(sequence_count, SEQUENCE_TOKENS, KEY_VALUE_HEADS, HEAD_DIM)))
    value_linear = low_back(jnp.dot(normed, value_weight, precision=HIGHEST))
    value_token_rows = low(value_linear).reshape(sequence_count, SEQUENCE_TOKENS, KEY_VALUE_HEADS, HEAD_DIM)
    attended = lax.map(jax.checkpoint(attend_one), (queries, key_token_rows, value_token_rows, segment_rows))
    attended = low_back(low(attended.reshape(token_count, QUERY_HEADS * HEAD_DIM)))
    hidden = values_in + low_back(jnp.dot(attended, w_out, precision=HIGHEST))
    mixer_in = low(rms_norm(hidden, mixer_gain))
    experts = w_gate.shape[0]
    picked = (route_now[:, :, None] == jnp.arange(experts, dtype=jnp.int32)[None, None, :]).astype(jnp.float32)
    shares = lax.optimization_barrier(jnp.sum(gate_now[:, :, None] * picked, axis=1))

    def expert_step(carried, packed):
        gate_mat, up_mat, down_mat, share_col = packed
        gate_lin = low_back(jnp.dot(mixer_in, gate_mat, precision=HIGHEST))
        up_lin = low_back(jnp.dot(mixer_in, up_mat, precision=HIGHEST))
        activation = low(jax.nn.silu(gate_lin) * up_lin)
        expert_out = low_back(low(jnp.dot(activation, down_mat, precision=HIGHEST)))
        return (carried + share_col[:, None] * expert_out, None)
    mixture, _ = lax.scan(jax.checkpoint(expert_step), jnp.zeros_like(hidden), (w_gate, w_up, w_down, shares.T))
    return hidden + mixture

def reference(inputs, cotangent, segments, routes, route_gates, attn_gain, w_query, key_weight, value_weight, w_out, mixer_gain, w_gate, w_up, w_down):
    micro_count = inputs.shape[0]
    model_width = inputs.shape[2]
    token_count = inputs.shape[0] * inputs.shape[1]
    segment_rows = segments.reshape(-1, segments.shape[-1])
    flat_routes = routes.reshape(routes.shape[0], token_count, -1)
    flat_gates = route_gates.reshape(route_gates.shape[0], token_count, -1).astype(jnp.float32)

    def forward(values_in, section_probe, gain_one, query_mat, key_mat, value_mat, out_mat, gain_two, gate_mats, up_mats, down_mats):
        first_out = layer_apply(values_in, segment_rows, flat_routes[0], flat_gates[0], gain_one[0], query_mat[0], key_mat[0], value_mat[0], out_mat[0], gain_two[0], gate_mats[0], up_mats[0], down_mats[0])
        section_in = low_back(low(first_out)) + section_probe
        second_out = layer_apply(section_in, segment_rows, flat_routes[1], flat_gates[1], gain_one[1], query_mat[1], key_mat[1], value_mat[1], out_mat[1], gain_two[1], gate_mats[1], up_mats[1], down_mats[1])
        return (second_out, first_out)
    primal, pull_back, first_out = jax.vjp(forward, inputs.reshape(token_count, model_width).astype(jnp.float32), jnp.zeros((token_count, model_width), jnp.float32), attn_gain.astype(jnp.float32), w_query.astype(jnp.float32), key_weight.astype(jnp.float32), value_weight.astype(jnp.float32), w_out.astype(jnp.float32), mixer_gain.astype(jnp.float32), w_gate.astype(jnp.float32), w_up.astype(jnp.float32), w_down.astype(jnp.float32), has_aux=True)
    gradients = pull_back(cotangent.reshape(token_count, model_width).astype(jnp.float32))
    layer_outputs = jnp.stack([first_out, primal]).astype(jnp.bfloat16).reshape(2, micro_count, -1, model_width)
    input_grads = jnp.stack([gradients[0], gradients[1]]).reshape(2, micro_count, -1, model_width)
    return (layer_outputs, input_grads, gradients[2], gradients[3], gradients[4], gradients[5], gradients[6], gradients[7], gradients[8], gradients[9], gradients[10])
```

```python
import jax
import jax.numpy as jnp
from jax import lax
from jax.sharding import PartitionSpec as P

S, D, T = "section", "dp", "tensor"
ST = (T, S)
HEADS = 12
GROUPS = 2
HEAD = 128
EPSILON = 1e-06
BF = jnp.bfloat16
F32 = jnp.float32


def dot(a, b, ca, cb):
    return lax.dot_general(a, b, ((ca, cb), ((), ())), preferred_element_type=F32)


def partner(values):
    return lax.ppermute(values, S, [(0, 1), (1, 0)])


def both(first, own):
    other = partner(own)
    return jnp.where(first, own, other), jnp.where(first, other, own)


def halves(first, own):
    keep = jnp.where(first, own[0], own[1])
    got = partner(jnp.where(first, own[1], own[0]))
    return jnp.where(first, keep, got), jnp.where(first, got, keep)


def join(first, zero, one):
    keep = jnp.where(first, zero, one)
    got = partner(jnp.where(first, one, zero))
    return jnp.stack([jnp.where(first, keep, got), jnp.where(first, got, keep)])


def rope_tables(places):
    half = HEAD // 2
    rates = 10000.0 ** (-jnp.arange(half, dtype=F32) * 2.0 / HEAD)
    angles = places[:, None] * rates[None, :]
    cosine, sine = jnp.cos(angles), jnp.sin(angles)
    return jnp.concatenate([cosine, cosine], 1)[:, None], jnp.concatenate([-sine, sine], 1)[:, None]


def rotate(values, cosine, sine):
    half = HEAD // 2
    turned = jnp.concatenate([values[..., half:], values[..., :half]], -1)
    return values * cosine + turned * sine


def inverse_rms(values):
    return lax.rsqrt(jnp.mean(values * values, -1, keepdims=True) + EPSILON)


def norm_back(grad, values, gain):
    r = inverse_rms(values)
    n = values * r
    m = grad * gain
    return r * (m - n * jnp.mean(m * n, -1, keepdims=True)), jnp.sum(grad * n, 0)


def scores_of(queries, keys, allowed):
    scores = dot(queries, keys, (2,), (1,)) * HEAD ** (-0.5)
    return jnp.where(allowed[None], scores, -1e30)


def attend(queries, keys, values, allowed):
    outs, logs = [], []
    per = HEADS // GROUPS
    for g in range(GROUPS):
        scores = scores_of(queries[g * per : (g + 1) * per], keys[:, g], allowed)
        peak = jnp.max(scores, -1, keepdims=True)
        raised = jnp.exp(scores - peak)
        total = jnp.sum(raised, -1, keepdims=True)
        probs = (raised / total).astype(BF)
        outs.append(dot(probs, values[:, g], (2,), (0,)).astype(BF))
        logs.append(peak + jnp.log(total))
    return jnp.concatenate(outs), jnp.concatenate(logs)


def attend_back(queries, keys, values, allowed, logs, grad_out):
    per = HEADS // GROUPS
    scale = HEAD ** (-0.5)
    gq, gk, gv = [], [], []
    for g in range(GROUPS):
        part = slice(g * per, (g + 1) * per)
        q, go = queries[part], grad_out[part]
        soft = jnp.exp(scores_of(q, keys[:, g], allowed) - logs[part])
        grad_probs = dot(go, values[:, g], (2,), (1,))
        inner = jnp.sum(soft * grad_probs, -1, keepdims=True)
        gs = (soft * (grad_probs - inner)).astype(BF)
        gq.append(dot(gs, keys[:, g], (2,), (0,)) * scale)
        gk.append(dot(gs, q, (0, 1), (0, 1)) * scale)
        gv.append(dot(soft.astype(BF), go, (0, 1), (0, 1)))
    return jnp.concatenate(gq), jnp.stack(gk, 1), jnp.stack(gv, 1)


def layer_forward(x, p, c, last):
    rows, width = x.shape
    xf = x.astype(F32)
    normed = (xf * inverse_rms(xf) * p["ga"]).astype(BF)
    kv = dot(normed, p["kv"], (1,), (0,)).reshape(rows, 2 * GROUPS, HEAD)
    keys = rotate(kv[:, :GROUPS], *c["rope"])
    kv = jnp.concatenate([keys, kv[:, GROUPS:]], 1).astype(BF)
    kv = lax.all_gather(kv.reshape(rows, -1), T, axis=0, tiled=True).reshape(-1, 2 * GROUPS, HEAD)
    keys, values = kv[:, :GROUPS], kv[:, GROUPS:]
    queries = dot(normed, p["wq"], (1,), (1,)).reshape(rows, HEADS, HEAD)
    queries = rotate(queries, *c["rope"]).astype(BF).transpose(1, 0, 2)
    attended, logs = attend(queries, keys, values, c["allowed"])
    flat = attended.transpose(1, 0, 2).reshape(rows, HEADS * HEAD)
    hidden = xf + dot(flat, p["wo"], (1,), (0,))
    mixer = (hidden * inverse_rms(hidden) * p["gm"]).astype(BF)
    tokens = lax.all_gather(mixer, D, axis=0, tiled=True)
    gate = dot(tokens, p["wg"], (1,), (3,))
    up = dot(tokens, p["wu"], (1,), (3,))
    act = (jax.nn.silu(gate) * up * p["share"]).astype(BF)
    part = dot(act, p["wd"], (1, 2, 3), (0, 1, 2)).astype(BF)
    y = hidden + lax.psum_scatter(part, D, scatter_dimension=0, tiled=True).astype(F32)
    kept = dict(
        xf=xf, normed=normed, keys=keys, values=values, queries=queries, logs=logs, flat=flat,
        hidden=hidden, tokens=tokens, gate=gate, up=up, act=act,
    )
    return y.astype(BF), kept


def layer_backward(grad, grad_all, k, p, c):
    rows, width = grad.shape
    gate, up, share = k["gate"], k["up"], p["share"]
    grad_act = dot(grad_all, p["wd"], (1,), (3,)) * share
    gw_down = dot(k["act"], grad_all, (0,), (0,)).astype(BF)
    sig = jax.nn.sigmoid(gate)
    grad_gate = (grad_act * up * sig * (1.0 + gate * (1.0 - sig))).astype(BF)
    grad_up = (grad_act * gate * sig).astype(BF)
    mixed = dot(grad_gate, p["wg"], (1, 2, 3), (0, 1, 2)) + dot(grad_up, p["wu"], (1, 2, 3), (0, 1, 2))
    gw_gate = dot(grad_gate, k["tokens"], (0,), (0,)).astype(BF)
    gw_up = dot(grad_up, k["tokens"], (0,), (0,)).astype(BF)
    grad_mixer = lax.psum_scatter(mixed.astype(BF), D, scatter_dimension=0, tiled=True).astype(F32)
    more, g_gm = norm_back(grad_mixer, k["hidden"], p["gm"])
    grad_hidden = grad + more
    gao = grad_hidden.astype(BF)
    gw_out = dot(k["flat"], gao, (0,), (0,)).astype(BF)
    ga = dot(gao, p["wo"], (1,), (1,)).astype(BF).reshape(rows, HEADS, HEAD).transpose(1, 0, 2)
    gq, gk, gv = attend_back(k["queries"], k["keys"], k["values"], c["allowed"], k["logs"], ga)
    gkv = jnp.concatenate([gk, gv], 1).astype(BF).reshape(-1, 2 * GROUPS * HEAD)
    gkv = lax.psum_scatter(gkv, T, scatter_dimension=0, tiled=True).astype(F32)
    gkv = gkv.reshape(rows, 2 * GROUPS, HEAD)
    cosine, sine = c["rope"]
    gkv = jnp.concatenate([rotate(gkv[:, :GROUPS], cosine, -sine), gkv[:, GROUPS:]], 1)
    gkv = gkv.astype(BF).reshape(rows, -1)
    gql = rotate(gq.transpose(1, 0, 2), cosine, -sine).astype(BF).reshape(rows, p["wq"].shape[0], -1)
    grad_normed = dot(gql, p["wq"], (1, 2), (0, 2)) + dot(gkv, p["kv"], (1,), (1,))
    gw_q = dot(k["normed"], gql, (0,), (0,)).transpose(1, 0, 2).astype(BF)
    gw_kv = dot(k["normed"], gkv, (0,), (0,))
    more, g_ga = norm_back(grad_normed, k["xf"], p["ga"])
    grads = dict(wd=gw_down, wg=gw_gate, wu=gw_up, wo=gw_out, wq=gw_q, kv=gw_kv, gm=g_gm, ga=g_ga)
    return grad_hidden + more, grads


def on_device(
    inputs, cotangent, segments, routes, route_gates, attn_gain, w_query, key_weight,
    value_weight, w_out, mixer_gain, w_gate, w_up, w_down,
):
    section = lax.axis_index(S)
    first = section == 0
    at = lax.axis_index(T)
    group = lax.axis_size(T)
    rows, width = inputs.shape[1:]
    length = segments.shape[2]
    here = w_gate.shape[1]
    hidden = w_gate.shape[3]
    experts = lax.axis_size(D) * here
    pick = lambda a: jnp.where(first, a[0], a[1])
    x0 = pick(inputs)
    grad1 = pick(cotangent)
    segment = pick(segments)[0]

    named = routes[0][..., None] == jnp.arange(experts, dtype=jnp.int32)
    shares = jnp.sum(jnp.where(named, route_gates[0][..., None], 0.0), 2)
    keep = jnp.where(first, shares[0], shares[1])
    got = partner(jnp.where(first, shares[1], shares[0]))
    shares = jnp.stack([jnp.where(first, keep, got), jnp.where(first, got, keep)], 1)
    shares = lax.all_gather(shares, D, axis=0, tiled=True)
    shares = lax.dynamic_slice_in_dim(shares, lax.axis_index(D) * here, here, 2)

    queries_at = at * rows + jnp.arange(rows)
    mine = lax.dynamic_slice_in_dim(segment, at * rows, rows, 0)
    allowed = (jnp.arange(length)[None] <= queries_at[:, None]) & (mine[:, None] == segment[None])
    c = dict(rope=rope_tables(queries_at.astype(F32)), allowed=allowed)

    gather = lambda a: lax.all_gather(a, ST, axis=0, tiled=False)
    wq = halves(first, w_query[0].reshape(2, width // 2, -1))
    wo = halves(first, w_out[0].reshape(2, -1, width))
    g, u = (w[0].transpose(0, 2, 1) for w in (w_gate, w_up))
    ffn = halves(first, jnp.stack([g, u, w_down[0]], 1))
    kv = both(first, jnp.concatenate([key_weight[0], value_weight[0]], 1))
    ga = both(first, attn_gain)
    gm = both(first, mixer_gain)
    params = []
    for l in range(2):
        f = gather(ffn[l]).reshape(group, here, 3, hidden, width)
        q = gather(wq[l]).reshape(group, width, -1)
        o = gather(wo[l]).reshape(-1, width)
        share = shares[:, l]
        params.append(
            dict(
                wq=q, wo=o, kv=kv[l], ga=ga[l], gm=gm[l], wg=f[:, :, 0], wu=f[:, :, 1], wd=f[:, :, 2],
                share=share[:, None, :, None],
            )
        )
    y0, k0 = layer_forward(x0, params[0], c, False)
    y1, k1 = layer_forward(y0, params[1], c, True)
    spread = lambda a: lax.all_gather(a.astype(BF), D, axis=0, tiled=True)
    gx1, w1 = layer_backward(grad1, spread(grad1), k1, params[1], c)
    gb = gx1.astype(BF)
    gx0, w0 = layer_backward(gb.astype(F32), spread(gb), k0, params[0], c)

    def swap(zero, one):
        keep = jnp.where(first, zero, one)
        got = partner(jnp.where(first, one, zero))
        return jnp.stack([jnp.where(first, keep, got), jnp.where(first, got, keep)])

    outs = swap(y0, y1)
    input_grads = swap(gx0.astype(BF), gx1.astype(BF)).astype(F32)
    scatter = lambda a: lax.psum_scatter(a, ST, scatter_dimension=0, tiled=True)
    reduced = []
    for w in (w0, w1):
        f = jnp.stack([w["wg"], w["wu"], w["wd"]], 2)
        f = scatter(f.reshape(group * here, 3, hidden, width)).reshape(3, hidden, width)
        q = scatter(w["wq"].reshape(group * 2, width // 2, -1)).reshape(width // 2, -1)
        o = scatter(w["wo"].reshape(group * 2, -1, width)).reshape(-1, width)
        reduced.append((f, q, o))
    f, q, o = (join(first, a, b) for a, b in zip(*reduced))
    q, o = lax.psum((q.reshape(w_query.shape[1:]), o.reshape(w_out.shape[1:])), D)
    small = [jnp.where(first, w0[n], w1[n]) + partner(jnp.where(first, w1[n], w0[n])) for n in ("kv", "ga", "gm")]
    kv, ga, gm = lax.psum(tuple(small), (D, T))
    f = f.astype(F32)
    half = kv.shape[1] // 2
    return (
        outs[None], input_grads[None], ga.reshape(1, -1), q.astype(F32)[None], kv[None, :, :half],
        kv[None, :, half:], o.astype(F32)[None], gm.reshape(1, -1), f[:, 0].transpose(0, 2, 1)[None],
        f[:, 1].transpose(0, 2, 1)[None], f[:, 2][None],
    )


def solution(mesh):
    rows, layer, cols = P(None, (D, T), None), P(S, None, (D, T), None), P(S, D, None, T)
    in_specs = (
        rows, rows, P(None, D, None), layer, layer, P(S, None), P(S, None, T), P(S, None, None),
        P(S, None, None), P(S, T, None), P(S, None), cols, cols, P(S, D, T, None),
    )
    out_specs = (
        layer, layer, P(S, None), P(S, None, T), P(S, None, None), P(S, None, None), P(S, T, None),
        P(S, None), cols, cols, P(S, D, T, None),
    )
    return jax.shard_map(on_device, mesh=mesh, in_specs=in_specs, out_specs=out_specs, check_vma=False)
```

```python
import functools
import jax
import jax.numpy as jnp
from jax import lax
from jax.experimental import pallas as pl
from jax.experimental.pallas import tpu as pltpu
from jax.sharding import PartitionSpec as P

S, D, T = "section", "dp", "tensor"
HEADS = 12
GROUPS = 2
HEAD = 128
EPSILON = 1e-06
BF = jnp.bfloat16
F32 = jnp.float32


def dot(a, b, ca, cb):
    return lax.dot_general(a, b, ((ca, cb), ((), ())), preferred_element_type=F32)


def low(values):
    return lax.reduce_precision(values.astype(F32), 8, 7).astype(BF)


def partner(values):
    return lax.ppermute(values, S, [(0, 1), (1, 0)])


def both(first, own):
    other = partner(own)
    return jnp.where(first, own, other), jnp.where(first, other, own)


def swap(first, zero, one):
    keep = jnp.where(first, zero, one)
    got = partner(jnp.where(first, one, zero))
    return jnp.where(first, keep, got), jnp.where(first, got, keep)


def hop(values, bit):
    return lax.ppermute(values, T, [(i, i ^ bit) for i in range(lax.axis_size(T))])


def spread(piece, after):
    a, b = piece
    if after is not None:
        a, b, _ = lax.optimization_barrier((a, b, after))
    ax, by = hop(a, 1), hop(b, 2)
    ay = hop(jnp.stack([a, ax]), 2)
    bx = hop(jnp.stack([b, by]), 1)
    return [a, ax, ay[0], ay[1]], [b, bx[0], by, bx[1]], (ay, bx)


def add(*values):
    return low(sum(v.astype(F32) for v in values))


def reduce_spread(a, b):
    ra = hop(jnp.stack([a[1], a[3]]), 1)
    rb = hop(jnp.stack([b[2], b[3]]), 2)
    own_a = hop(add(a[2], ra[1]), 2)
    own_b = hop(add(b[1], rb[1]), 1)
    return add(a[0], ra[0], own_a), add(b[0], rb[0], own_b)


def sum_spread(a, b):
    a, b = add(a, hop(a, 1)), add(b, hop(b, 2))
    return add(a, hop(a, 2)), add(b, hop(b, 1))


def rope_tables(places):
    half = HEAD // 2
    rates = 10000.0 ** (-jnp.arange(half, dtype=F32) * 2.0 / HEAD)
    angles = places[:, None] * rates[None, :]
    cosine, sine = jnp.cos(angles), jnp.sin(angles)
    return jnp.concatenate([cosine, cosine], 1), jnp.concatenate([-sine, sine], 1)


def rotate(values, cosine, sine):
    half = HEAD // 2
    turned = jnp.concatenate([values[..., half:], values[..., :half]], -1)
    return values * cosine + turned * sine


def inverse_rms(values):
    return lax.rsqrt(jnp.mean(values * values, -1, keepdims=True) + EPSILON)


def norm_back(grad, values, gain):
    r = inverse_rms(values)
    n = values * r
    m = grad * gain
    return r * (m - n * jnp.mean(m * n, -1, keepdims=True)), jnp.sum(grad * n, 0)


MESH = pl.DeviceIdType.MESH
SMALL = 4
SUB = 4
VMEM_LIMIT = 48 * 1024 * 1024


def expert_kernel(n, forward, backward, *refs):
    refs = list(refs)
    take = lambda count: [refs.pop(0) for _ in range(count)]
    x, mine, other, share = take(4)
    grads_in = take(1)[0] if forward and backward else None
    saved = take(4) if not forward else None
    y = take(1)[0]
    outs = take(4) if not backward else None
    part_out = take(1)[0] if forward and backward else None
    gw_out = take(1)[0] if backward else None
    tok, part, got, w, gate, up, act = take(7)
    second = take(1)[0] if backward else None
    stage = take(1)[0] if backward else None
    tok_send, tok_recv, part_send, part_recv, w_sem, io_sem, save_sem = refs
    rows, width = x.shape
    sub = rows // SUB
    me = lax.axis_index(D)

    small = mine.shape[3]
    for i in range(3):
        for h, pieces in enumerate((mine, other)):
            for p in range(2):
                for r in range(4):
                    at = ((h * 2 + p) * 4 + r) * small
                    pltpu.make_async_copy(pieces.at[p, r, i], w.at[i, pl.ds(at, small)], w_sem.at[i]).start()
    loads = []
    if saved is not None:
        loads = [pltpu.make_async_copy(a, o, io_sem.at[i]) for i, (a, o) in enumerate(zip(saved, (gate, up, act, second)))]
    elif backward:
        loads = [pltpu.make_async_copy(grads_in, second, io_sem.at[0])]
    for load in loads:
        load.start()
    barrier = pltpu.get_barrier_semaphore()
    for step in (-1, 1):
        @pl.when((me + step >= 0) & (me + step < n))
        def _():
            pl.semaphore_signal(barrier, inc=1, device_id={D: me + step}, device_id_type=MESH)
    tok[me] = x[...]
    pl.semaphore_wait(barrier, jnp.where((me == 0) | (me == n - 1), 1, 2))

    def move(b, to, side):
        return pltpu.make_async_remote_copy(
            src_ref=tok.at[b], dst_ref=tok.at[b], send_sem=tok_send.at[side, b], recv_sem=tok_recv.at[b],
            device_id={D: to}, device_id_type=MESH,
        )

    def pass_sum(b, s, to, slot):
        at = pl.ds(pl.multiple_of(s * sub, sub), sub)
        return pltpu.make_async_remote_copy(
            src_ref=part.at[b, at], dst_ref=got.at[slot, at], send_sem=part_send.at[b, s],
            recv_sem=part_recv.at[slot, s], device_id={D: to}, device_id_type=MESH,
        )

    def right(b, s):
        return pass_sum(b, s, me + 1, b)

    def left(b, s):
        return pass_sum(b, s, me - 1, jnp.where(b == me - 1, n, b))

    def arrived(b, s, slot):
        pass_sum(b, s, me, slot).wait_recv()

    chunk = 256
    steps = width // chunk

    def chunked(body):
        def step(c, carry):
            body(pl.ds(pl.multiple_of(c * chunk, chunk), chunk), c)
            return carry
        lax.fori_loop(0, steps, step, 0)

    def run(b):
        values = tok.at[b]

        def scale(c):
            s = share[c * 2 // steps, b]
            return jnp.concatenate([s, s], 1)

        if forward:
            def ahead(cols, c):
                gt = dot(values[...], w[0, cols], (1,), (1,))
                u = dot(values[...], w[1, cols], (1,), (1,))
                gate[b, :, cols] = gt.astype(BF)
                up[b, :, cols] = u.astype(BF)
                act[b, :, cols] = (gt * jax.nn.sigmoid(gt) * u * scale(c)).astype(BF)

            chunked(ahead)

            def down(cols, c):
                part[b, :, cols] = dot(act[b], w[2, :, cols], (1,), (0,)).astype(BF)

            chunked(down)
            if not backward:
                for i, (a, o) in enumerate(zip((tok, act, gate, up), outs)):
                    pltpu.make_async_copy(a.at[b], o.at[b], save_sem.at[i, b]).start()
            else:
                save = pltpu.make_async_copy(part.at[b], part_out.at[b], save_sem.at[0, b])
                save.start()
                save.wait()
        if backward:
            source = second.at[b] if forward else values

            def back(cols, c):
                da = dot(source[...], w[2, cols], (1,), (1,)) * scale(c)
                gt, u = gate[b, :, cols].astype(F32), up[b, :, cols].astype(F32)
                sig = jax.nn.sigmoid(gt)
                gate[b, :, cols] = (da * u * sig * (1.0 + gt * (1.0 - sig))).astype(BF)
                up[b, :, cols] = (da * gt * sig).astype(BF)

            chunked(back)

            def mix(cols, c):
                total = dot(gate[b], w[0, :, cols], (1,), (0,)) + dot(up[b], w[1, :, cols], (1,), (0,))
                part[b, :, cols] = total.astype(BF)

            chunked(mix)

    def turn(i, carry):
        d = (i + 1) // 2
        b = me + jnp.where(i % 2 == 1, d, -d)

        @pl.when((b >= 0) & (b < n))
        def _():
            @pl.when(i > 0)
            def _():
                move(b, me, 0).wait_recv()

            @pl.when((me < n - 1) & (b <= me))
            def _():
                move(b, me + 1, 0).start()

            @pl.when((me > 0) & (b >= me))
            def _():
                move(b, me - 1, 1).start()

            @pl.when(i == 0)
            def _():
                for k in range(3):
                    pltpu.make_async_copy(w.at[k], w.at[k], w_sem.at[k]).wait()
                for load in loads:
                    load.wait()

            run(b)

            @pl.when((b > me) & (me == 0))
            def _():
                for s in range(SUB):
                    right(b, s).start()

            @pl.when((b < me) & (me == n - 1))
            def _():
                for s in range(SUB):
                    left(b, s).start()

        return carry

    lax.fori_loop(0, 2 * n - 1, turn, 0)

    piece = 256
    slices = width // piece
    total = 3 * slices

    def save_slice(k, slot):
        at = pl.ds(pl.multiple_of(k % slices * piece, piece), piece)
        return pltpu.make_async_copy(stage.at[slot], gw_out.at[k // slices, at], save_sem.at[1, slot])

    def weight_slice(k):
        slot = k % 2
        at = pl.ds(pl.multiple_of(k % slices * piece, piece), piece)

        @pl.when(k >= 2)
        def _():
            save_slice(k - 2, slot).wait()

        tokens, grads = (tok, second) if forward else (second, tok)
        for i, (a, v) in enumerate(((gate, tokens), (up, tokens), (act, grads))):
            @pl.when(k // slices == i)
            def _():
                lhs = jnp.concatenate([a[b, :, at] for b in range(n)], 0)
                for c in range(2):
                    cols = pl.ds(c * (width // 2), width // 2)
                    rhs = jnp.concatenate([v[b, :, cols] for b in range(n)], 0)
                    stage[slot, :, cols] = dot(lhs, rhs, (0,), (0,)).astype(BF)

        save_slice(k, slot).start()

    def add_rows(b, s, slot):
        at = pl.ds(pl.multiple_of(s * sub, sub), sub)
        part[b, at] = (part[b, at].astype(F32) + got[slot, at].astype(F32)).astype(BF)

    count = (n - 1) * SUB

    def relay(t, carry):
        q, s = 1 + t // SUB, t % SUB

        @pl.when((me > 0) & (q > me))
        def _():
            arrived(q, s, q)
            add_rows(q, s, q)
            right(q, s).start()

        @pl.when((me < n - 1) & (n - 1 - q < me))
        def _():
            b = n - 1 - q
            arrived(b, s, b)
            add_rows(b, s, b)
            left(b, s).start()

        if backward:
            def some(k, carry):
                weight_slice(k)
                return carry
            lax.fori_loop(t * total // count, (t + 1) * total // count, some, 0)
        return carry

    lax.fori_loop(0, count, relay, 0)
    y[...] = part[me].astype(F32)

    @pl.when(me > 0)
    def _():
        for s in range(SUB):
            arrived(me, s, me)
        y[...] += got[me].astype(F32)

    @pl.when(me < n - 1)
    def _():
        for s in range(SUB):
            arrived(me, s, n)
        y[...] += got[n].astype(F32)

    if backward:
        for k in (total - 2, total - 1):
            save_slice(k, k % 2).wait()
    for b in range(n):
        if not backward:
            for i, (a, o) in enumerate(zip((tok, act, gate, up), outs)):
                pltpu.make_async_copy(a.at[b], o.at[b], save_sem.at[i, b]).wait()

        @pl.when((me < n - 1) & (b <= me))
        def _():
            move(b, me + 1, 0).wait_send()

        @pl.when((me > 0) & (b >= me))
        def _():
            move(b, me - 1, 1).wait_send()

        @pl.when(b > me)
        def _():
            for s in range(SUB):
                right(b, s).wait_send()

        @pl.when(b < me)
        def _():
            for s in range(SUB):
                left(b, s).wait_send()


def experts(n, forward, backward, x, mine, other, share, *more):
    rows, width = x.shape
    hidden = mine.shape[3] * 16
    shape = lambda *dims: jax.ShapeDtypeStruct(dims, BF)
    whole, wide = shape(n, rows, width), shape(n, rows, hidden)
    out = [jax.ShapeDtypeStruct((rows, width), F32)]
    out += [] if backward else [whole, wide, wide, wide]
    out += [whole] if forward and backward else []
    out += [shape(3, hidden, width)] if backward else []
    room = lambda *dims: pltpu.VMEM(dims, BF)
    scratch = [room(n, rows, width), room(n, rows, width), room(n + 1, rows, width), room(3, hidden, width)]
    scratch += [room(n, rows, hidden)] * 3
    scratch += [room(n, rows, width), room(2, 256, width)] if backward else []
    dma = pltpu.SemaphoreType.DMA
    scratch += [dma((2, n)), dma((n,)), dma((n, SUB)), dma((n + 1, SUB)), dma((3,)), dma((4,)), dma((4, n))]
    vmem, far = pl.BlockSpec(memory_space=pltpu.VMEM), pl.BlockSpec(memory_space=pl.ANY)
    return pl.pallas_call(
        functools.partial(expert_kernel, n, forward, backward),
        out_shape=out,
        in_specs=[vmem, far, far, vmem] + [far] * len(more),
        out_specs=[vmem] + [far] * (len(out) - 1),
        scratch_shapes=scratch,
        compiler_params=pltpu.CompilerParams(
            collective_id=forward + 2 * backward, has_side_effects=True, vmem_limit_bytes=VMEM_LIMIT
        ),
        cost_estimate=pl.CostEstimate(flops=80 * 10**9, bytes_accessed=10**8, transcendentals=0),
    )(x, mine, other, share, *more)


def turn_head(values, cosine, sine):
    return values * cosine + pltpu.roll(values, HEAD // 2, 1) * sine


def head_group(i):
    own = i // 3
    return jnp.where(lax.axis_index(T) < 2, own, 1 - own)


def lanes(start, size=HEAD):
    return pl.ds(pl.multiple_of(start, HEAD), size)


def loop(count, body):
    def step(i, carry):
        body(i)
        return carry
    lax.fori_loop(0, count, step, 0)


def attend_kernel(x, normed, kv, bias, cosine, sine, wq, wo, gain, hidden, mixer, queries, flat, logs):
    pair = 2 * HEAD

    def heads(i):
        both = dot(normed[...], wq[lanes(i * pair, pair)], (1,), (1,))
        g = head_group(i)
        keys, values = kv[:, lanes(g * HEAD)], kv[:, lanes((GROUPS + g) * HEAD)]
        for j in range(2):
            at = lanes(i * pair + j * HEAD)
            q = turn_head(both[:, j * HEAD : (j + 1) * HEAD], cosine[...], sine[...]).astype(BF)
            queries[:, at] = q
            scores = dot(q, keys, (1,), (1,)) * HEAD ** (-0.5) + bias[...]
            peak = jnp.max(scores, 1, keepdims=True)
            raised = jnp.exp(scores - peak)
            total = jnp.sum(raised, 1, keepdims=True)
            probs = (raised * (1.0 / total)).astype(BF)
            flat[:, at] = dot(probs, values, (1,), (0,)).astype(BF)
            logs[:, at] = jnp.broadcast_to(peak + jnp.log(total), q.shape)

    loop(HEADS // 2, heads)

    def out(i):
        cols = lanes(i * pair, pair)
        hidden[:, cols] = x[:, cols].astype(F32) + dot(flat[...], wo[:, cols], (1,), (0,))

    loop(x.shape[1] // pair, out)
    h = hidden[...]
    mixer[...] = (h * inverse_rms(h) * gain[...]).astype(BF)


def attend_back_kernel(
    grad, grad_mixer, hidden, gain, wo, queries, kv, logs, bias, flat, cosine, sine,
    grad_hidden, gql, gkv, gwo, grad_gain, gao, ga, acc,
):
    pair = 2 * HEAD
    scale = HEAD ** (-0.5)
    h = hidden[...]
    r = inverse_rms(h)
    n = h * r
    grad_gain[...] = jnp.sum(grad_mixer[...] * n, 0, keepdims=True)
    m = grad_mixer[...] * gain[...]
    total = grad[...] + r * (m - n * jnp.mean(m * n, -1, keepdims=True))
    grad_hidden[...] = total
    gao[...] = total.astype(BF)
    acc[...] = jnp.zeros_like(acc)

    def heads(i):
        rows = lanes(i * pair, pair)
        ga[...] = dot(gao[...], wo[rows], (1,), (1,)).astype(BF)
        gwo[rows] = dot(flat[:, rows], gao[...], (0,), (0,)).astype(BF)
        g = head_group(i)
        key_at, value_at = lanes(g * HEAD), lanes((GROUPS + g) * HEAD)
        keys, values = kv[:, key_at], kv[:, value_at]
        for j in range(2):
            at = lanes(i * pair + j * HEAD)
            q, go = queries[:, at], ga[:, j * HEAD : (j + 1) * HEAD]
            scores = dot(q, keys, (1,), (1,)) * scale + bias[...]
            soft = jnp.exp(scores - logs[:, at][:, :1])
            grad_probs = dot(go, values, (1,), (1,))
            inner = jnp.sum(soft * grad_probs, 1, keepdims=True)
            gs = (soft * (grad_probs - inner)).astype(BF)
            gq = dot(gs, keys, (1,), (0,)) * scale
            gql[:, at] = turn_head(gq, cosine[...], -sine[...]).astype(BF)
            acc[:, key_at] += dot(gs, q, (0,), (0,)) * scale
            acc[:, value_at] += dot(soft.astype(BF), go, (0,), (0,))

    loop(HEADS // 2, heads)
    gkv[...] = acc[...].astype(BF)


def local_call(body, flops, out, scratch, *operands):
    return pl.pallas_call(
        body,
        out_shape=[jax.ShapeDtypeStruct(*o) for o in out],
        scratch_shapes=[pltpu.VMEM(*s) for s in scratch],
        compiler_params=pltpu.CompilerParams(vmem_limit_bytes=VMEM_LIMIT),
        cost_estimate=pl.CostEstimate(flops=flops, bytes_accessed=2 * 10**7, transcendentals=0),
    )(*operands)


def attention_forward(x, p, c):
    rows, width = x.shape
    xf = x.astype(F32)
    normed = low(xf * inverse_rms(xf) * p["ga"])
    kv = dot(normed, p["kv"], (1,), (0,)).reshape(rows, 2 * GROUPS, HEAD)
    cosine, sine = c["rope"]
    keys = rotate(kv[:, :GROUPS], cosine[:, None], sine[:, None])
    kv = low(jnp.concatenate([keys, kv[:, GROUPS:]], 1)).reshape(rows, -1)
    kv = jnp.concatenate([kv] + [hop(kv, r) for r in (1, 2, 3)])
    wide = (rows, HEADS * HEAD)
    hidden, mixer, queries, flat, logs = local_call(
        attend_kernel, 10**10, [((rows, width), F32), ((rows, width), BF), (wide, BF), (wide, BF), (wide, F32)], [],
        x, normed, kv, c["bias"], cosine, sine, p["wq"], p["wo"], p["gm"].reshape(1, -1),
    )
    kept = dict(x=x, normed=normed, kv=kv, queries=queries, logs=logs, flat=flat, hidden=hidden)
    return hidden, mixer, kept


def along(values):
    return lax.all_gather(low(values), D, axis=0, tiled=True)


def scatter_along(values):
    return lax.psum_scatter(low(values.reshape(-1, values.shape[-1])), D, scatter_dimension=0, tiled=True)


def weights_of(p):
    f = jnp.stack([p["mine"], p["other"]])
    return tuple(f[:, :, :, i].reshape(-1, f.shape[-1]) for i in range(3))


def share_of(p, hidden):
    return jnp.repeat(p["share"], hidden // 2, axis=1)


def mix_forward(mixer, p, n):
    if n <= SMALL:
        y, tokens, act, gate, up = experts(n, True, False, mixer, p["mine"], p["other"], p["wide"])
        return y, dict(tokens=tokens, act=act, gate=gate, up=up)
    wg, wu, wd = weights_of(p)
    tokens = along(mixer)
    gate, up = dot(tokens, wg, (1,), (1,)), dot(tokens, wu, (1,), (1,))
    act = low((jax.nn.silu(gate) * up * share_of(p, wd.shape[0])))
    y = scatter_along(dot(act, wd, (1,), (0,))).astype(F32)
    return y, dict(tokens=tokens, act=act, gate=low(gate), up=low(up))


def mix_backward(grad, k, p, n):
    if n <= SMALL:
        saved = (k["gate"], k["up"], k["act"], k["tokens"])
        return experts(n, False, True, grad, p["mine"], p["other"], p["wide"], *saved)
    wg, wu, wd = weights_of(p)
    grads = along(grad)
    da = dot(grads, wd, (1,), (1,)) * share_of(p, wd.shape[0])
    gate, up = k["gate"].astype(F32), k["up"].astype(F32)
    sig = jax.nn.sigmoid(gate)
    dg, du = low((da * up * sig * (1.0 + gate * (1.0 - sig)))), low((da * gate * sig))
    gm = scatter_along(dot(dg, wg, (1,), (0,)) + dot(du, wu, (1,), (0,))).astype(F32)
    flat = lambda v: v.reshape(-1, v.shape[-1])
    pairs = ((dg, k["tokens"]), (du, k["tokens"]), (k["act"], grads))
    return gm, jnp.stack([low(dot(flat(u), flat(v), (0,), (0,))) for u, v in pairs])


def mix_both(mixer, grad, p, n):
    if n <= SMALL:
        grads = along(grad).reshape(n, *grad.shape)
        gm, part, gw = experts(n, True, True, mixer, p["mine"], p["other"], p["wide"], grads)
        y = scatter_along(part).astype(F32)
        return y, gm, gw
    y, k = mix_forward(mixer, p, n)
    return (y,) + mix_backward(grad, k, p, n)


def expert_grads(gw):
    gw = gw.reshape(3, 2, 2, 4, -1, gw.shape[-1])
    gf = add(gw[:, 0], partner(gw[:, 1]))
    return reduce_spread(gf[:, 0].transpose(1, 0, 2, 3), gf[:, 1].transpose(1, 0, 2, 3))


def attention_backward(grad, grad_mixer, k, p, c, first):
    rows, width = grad.shape
    cosine, sine = c["rope"]
    wide, length = (rows, HEADS * HEAD), c["bias"].shape[1]
    grad_hidden, gql, gkv, gw_out, g_gm = local_call(
        attend_back_kernel, 2 * 10**10,
        [((rows, width), F32), (wide, BF), ((length, 2 * GROUPS * HEAD), BF), ((HEADS * HEAD, width), BF), ((1, width), F32)],
        [((rows, width), BF), ((rows, 2 * HEAD), BF), ((length, 2 * GROUPS * HEAD), F32)],
        grad, grad_mixer, k["hidden"], p["gm"].reshape(1, -1), p["wo"], k["queries"], k["kv"], k["logs"], c["bias"],
        k["flat"], cosine, sine,
    )
    gkv = gkv.reshape(4, rows, -1)
    gkv = gkv[0].astype(F32) + sum(hop(gkv[r], r).astype(F32) for r in (1, 2, 3))
    gkv = gkv.reshape(rows, 2 * GROUPS, HEAD)
    cosine, sine = cosine[:, None], sine[:, None]
    gkv = jnp.concatenate([rotate(gkv[:, :GROUPS], cosine, -sine), gkv[:, GROUPS:]], 1)
    gkv = low(gkv).reshape(rows, -1)
    grad_normed = dot(gql, p["wq"], (1,), (0,)) + dot(gkv, p["kv"], (1,), (1,))
    gw_q = low(dot(gql, k["normed"], (0,), (0,)))
    gw_kv = dot(gkv, k["normed"], (0,), (0,))
    more, g_ga = norm_back(grad_normed, k["x"].astype(F32), p["ga"])
    gat = add(jnp.where(first, gw_q, gw_out), partner(jnp.where(first, gw_out, gw_q)))
    gat = gat.reshape(4, 2, -1, width)
    gat = reduce_spread(gat[:, 0], gat[:, 1])
    gw_kv = gw_kv.reshape(2, -1, width)
    pad = jnp.zeros((31, width), F32)
    small = [low(jnp.concatenate([gw_kv[i], g[None], pad])) for i, g in enumerate((g_ga, g_gm[0]))]
    small = add(jnp.where(first, small[0], small[1]), partner(jnp.where(first, small[1], small[0])))
    small = small.reshape(2, -1, width)
    small = sum_spread(small[0], small[1])
    sums = lax.psum(jnp.concatenate(gat + small), D)
    return grad_hidden + more, sums


def on_device(
    inputs, cotangent, segments, routes, route_gates, attn_gain, w_query, key_weight,
    value_weight, w_out, mixer_gain, w_gate, w_up, w_down,
):
    section = lax.axis_index(S)
    first = section == 0
    at = lax.axis_index(T)
    rows, width = inputs.shape[1:]
    length = segments.shape[2]
    here = w_gate.shape[1]
    hidden = w_gate.shape[3]
    experts = lax.axis_size(D) * here
    mine = lambda a: lax.dynamic_index_in_dim(a, section, 0, False)
    theirs = lambda a: lax.dynamic_index_in_dim(a, 1 - section, 0, False)
    x0 = mine(inputs)
    grad1 = mine(cotangent)
    segment = mine(segments)[0]

    def halves(own):
        keep, got = mine(own), partner(theirs(own))
        return jnp.where(first, keep, got), jnp.where(first, got, keep)

    named = routes[0][..., None] == jnp.arange(experts, dtype=jnp.int32)
    shares = jnp.sum(jnp.where(named, route_gates[0][..., None], 0.0), 2)
    shares = jnp.stack(halves(shares), 1)
    shares = lax.all_gather(shares, D, axis=0, tiled=True)
    shares = lax.dynamic_slice_in_dim(shares, lax.axis_index(D) * here, here, 2)
    shares = jnp.where(first, shares, shares[:, :, ::-1])

    queries_at = at * rows + jnp.arange(rows)
    keys_at = jnp.concatenate([(at ^ r) * rows + jnp.arange(rows) for r in range(4)])
    key_segment = jnp.concatenate([lax.dynamic_slice_in_dim(segment, (at ^ r) * rows, rows, 0) for r in range(4)])
    allowed = (keys_at[None] <= queries_at[:, None]) & (key_segment[:rows, None] == key_segment[None])
    c = dict(rope=rope_tables(queries_at.astype(F32)), bias=jnp.where(allowed, 0.0, -1e30))

    attn = halves(jnp.stack([w_query[0].T, w_out[0]]).reshape(2, 2, -1, width))
    g, u = (w[0].transpose(0, 2, 1) for w in (w_gate, w_up))
    ffn = jnp.stack([g, u, w_down[0]], 1).reshape(here, 3, 2, -1, width).transpose(0, 2, 1, 3, 4)
    ffn = halves(ffn)
    kv = both(first, jnp.concatenate([key_weight[0], value_weight[0]], 1))
    ga = both(first, attn_gain)
    gm = both(first, mixer_gain)
    params = []
    after = None
    for l in range(2):
        a, b, after = spread(attn[l], after)
        got = jnp.concatenate([v for pair in zip(a, b) for v in pair])
        other = partner(got)
        q, o = jnp.where(first, got, other), jnp.where(first, other, got)
        a, b, after = spread(ffn[l], after)
        got = jnp.stack([jnp.stack(a), jnp.stack(b)])
        share = shares[:, l]
        wide = jnp.broadcast_to(share.T.reshape(here, -1, rows, 1), (here, share.shape[0] // rows, rows, HEAD))
        params.append(
            dict(wq=q, wo=o, kv=kv[l], ga=ga[l], gm=gm[l], mine=got, other=partner(got), share=share, wide=wide)
        )
    n = lax.axis_size(D)
    hidden0, mixer, k0 = attention_forward(x0, params[0], c)
    y, kept = mix_forward(mixer, params[0], n)
    y0 = low((hidden0 + y))
    hidden1, mixer, k1 = attention_forward(y0, params[1], c)
    y, gm, gw = mix_both(mixer, low(grad1), params[1], n)
    y1 = low((hidden1 + y))
    f1 = expert_grads(gw)
    gx1, s1 = attention_backward(grad1, gm, k1, params[1], c, first)
    gb = low(gx1)
    gm, gw = mix_backward(gb, kept, params[0], n)
    f0 = expert_grads(gw)
    gx0, s0 = attention_backward(gb.astype(F32), gm, k0, params[0], c, first)

    outs = jnp.stack(swap(first, y0, y1))
    input_grads = jnp.stack(swap(first, low(gx0), low(gx1))).astype(F32)
    f = jnp.stack(swap(first, jnp.concatenate(f0, 1), jnp.concatenate(f1, 1))).astype(F32)
    zero, one = swap(first, s0, s1)
    high = w_out.shape[1]
    q, o = zero[:high].astype(F32), one[:high].astype(F32)
    ka, vm = zero[high:].astype(F32), one[high:].astype(F32)
    few = GROUPS * HEAD
    return (
        outs[None], input_grads[None], ka[few : few + 1], q.T[None], ka[:few].T[None],
        vm[:few].T[None], o[None], vm[few : few + 1], f[:, 0].transpose(0, 2, 1)[None],
        f[:, 1].transpose(0, 2, 1)[None], f[:, 2][None],
    )


def solution(mesh):
    rows, layer, cols = P(None, (D, T), None), P(S, None, (D, T), None), P(S, D, None, T)
    in_specs = (
        rows, rows, P(None, D, None), layer, layer, P(S, None), P(S, None, T), P(S, None, None),
        P(S, None, None), P(S, T, None), P(S, None), cols, cols, P(S, D, T, None),
    )
    out_specs = (
        layer, layer, P(S, None), P(S, None, T), P(S, None, None), P(S, None, None), P(S, T, None),
        P(S, None), cols, cols, P(S, D, T, None),
    )
    return jax.shard_map(on_device, mesh=mesh, in_specs=in_specs, out_specs=out_specs, check_vma=False)
```

```python
import functools
import jax
import jax.numpy as jnp
from jax import lax
from jax.experimental import pallas as pl
from jax.experimental.pallas import tpu as pltpu
from jax.sharding import PartitionSpec as P

S, D, T = "section", "dp", "tensor"
HEADS = 12
GROUPS = 2
HEAD = 128
EPSILON = 1e-06
BF = jnp.bfloat16
F32 = jnp.float32


def dot(a, b, ca, cb):
    return lax.dot_general(a, b, ((ca, cb), ((), ())), preferred_element_type=F32)


def low(values):
    return lax.reduce_precision(values.astype(F32), 8, 7).astype(BF)


def partner(values):
    return lax.ppermute(values, S, [(0, 1), (1, 0)])


def both(first, own):
    other = partner(own)
    return jnp.where(first, own, other), jnp.where(first, other, own)


def swap(first, zero, one):
    keep = jnp.where(first, zero, one)
    got = partner(jnp.where(first, one, zero))
    return jnp.where(first, keep, got), jnp.where(first, got, keep)


def hop(values, bit):
    return lax.ppermute(values, T, [(i, i ^ bit) for i in range(lax.axis_size(T))])


def after(values, *others):
    return lax.optimization_barrier((values, others))[0]


def line_gather(own):
    n, me = lax.axis_size(D), lax.axis_index(D)
    if n != SMALL:
        return lax.all_gather(own, D, axis=0, tiled=True)
    got = [own] + [lax.ppermute(own, D, [(i, i ^ r) for i in range(n)]) for r in range(1, n)]
    got = jnp.stack(got)
    return jnp.concatenate([lax.dynamic_index_in_dim(got, me ^ b, 0, False) for b in range(n)])


def pieces_of(own):
    return [own] + [hop(own, r) for r in (1, 2, 3)]


def add(*values):
    return low(sum(v.astype(F32) for v in values))


def summed(parts):
    return add(parts[0], *(hop(parts[r], r) for r in (1, 2, 3)))


def over_sections(keep, give):
    got = partner(give)
    return [add(keep[r], got[r]) for r in range(4)]


def rope_tables(places):
    half = HEAD // 2
    rates = 10000.0 ** (-jnp.arange(half, dtype=F32) * 2.0 / HEAD)
    angles = places[:, None] * rates[None, :]
    cosine, sine = jnp.cos(angles), jnp.sin(angles)
    return jnp.concatenate([cosine, cosine], 1), jnp.concatenate([-sine, sine], 1)


def rotate(values, cosine, sine):
    half = HEAD // 2
    turned = jnp.concatenate([values[..., half:], values[..., :half]], -1)
    return values * cosine + turned * sine


def inverse_rms(values):
    return lax.rsqrt(jnp.mean(values * values, -1, keepdims=True) + EPSILON)


def norm_back(grad, values, gain):
    r = inverse_rms(values)
    n = values * r
    m = grad * gain
    return r * (m - n * jnp.mean(m * n, -1, keepdims=True)), jnp.sum(grad * n, 0)


MESH = pl.DeviceIdType.MESH
SMALL = 4
SUB = 4
VMEM_LIMIT = 48 * 1024 * 1024


def expert_kernel(n, forward, backward, *refs):
    refs = list(refs)
    take = lambda count: [refs.pop(0) for _ in range(count)]
    x, share = take(2)
    pieces = take(8)
    grads_in = take(1)[0] if forward and backward else None
    saved = take(4) if not forward else None
    y = take(1)[0]
    outs = take(4) if not backward else None
    part_out = take(1)[0] if forward and backward else None
    gw_outs = take(2) if backward else None
    tok, part, got, w, gate, up, act = take(7)
    second = take(1)[0] if backward else None
    stage = take(1)[0] if backward else None
    tok_send, tok_recv, part_send, part_recv, w_sem, io_sem, save_sem = refs
    rows, width = x.shape
    sub = rows // SUB
    me = lax.axis_index(D)

    small = pieces[0].shape[1]
    for i in range(3):
        for k, one in enumerate(pieces):
            pltpu.make_async_copy(one.at[i], w.at[i, pl.ds(k * small, small)], w_sem.at[i]).start()
    loads = []
    if saved is not None:
        loads = [pltpu.make_async_copy(a, o, io_sem.at[i]) for i, (a, o) in enumerate(zip(saved, (gate, up, act, second)))]
    elif backward:
        loads = [pltpu.make_async_copy(grads_in, second, io_sem.at[0])]
    for load in loads:
        load.start()
    barrier = pltpu.get_barrier_semaphore()
    for step in (-1, 1):
        @pl.when((me + step >= 0) & (me + step < n))
        def _():
            pl.semaphore_signal(barrier, inc=1, device_id={D: me + step}, device_id_type=MESH)
    tok[me] = x[...]
    pl.semaphore_wait(barrier, jnp.where((me == 0) | (me == n - 1), 1, 2))

    def move(b, to, side):
        return pltpu.make_async_remote_copy(
            src_ref=tok.at[b], dst_ref=tok.at[b], send_sem=tok_send.at[side, b], recv_sem=tok_recv.at[b],
            device_id={D: to}, device_id_type=MESH,
        )

    def pass_sum(b, s, to, slot):
        at = pl.ds(pl.multiple_of(s * sub, sub), sub)
        return pltpu.make_async_remote_copy(
            src_ref=part.at[b, at], dst_ref=got.at[slot, at], send_sem=part_send.at[b, s],
            recv_sem=part_recv.at[slot, s], device_id={D: to}, device_id_type=MESH,
        )

    def right(b, s):
        return pass_sum(b, s, me + 1, b)

    def left(b, s):
        return pass_sum(b, s, me - 1, jnp.where(b == me - 1, n, b))

    def arrived(b, s, slot):
        pass_sum(b, s, me, slot).wait_recv()

    chunk = 256
    steps = width // chunk

    def chunked(body):
        def step(c, carry):
            body(pl.ds(pl.multiple_of(c * chunk, chunk), chunk), c)
            return carry
        lax.fori_loop(0, steps, step, 0)

    def run(b):
        values = tok.at[b]

        def scale(c):
            s = share[c * 2 // steps, b]
            return jnp.concatenate([s, s], 1)

        if forward:
            def ahead(cols, c):
                gt = dot(values[...], w[0, cols], (1,), (1,))
                u = dot(values[...], w[1, cols], (1,), (1,))
                gate[b, :, cols] = gt.astype(BF)
                up[b, :, cols] = u.astype(BF)
                act[b, :, cols] = (gt * jax.nn.sigmoid(gt) * u * scale(c)).astype(BF)

            chunked(ahead)

            def down(cols, c):
                part[b, :, cols] = dot(act[b], w[2, :, cols], (1,), (0,)).astype(BF)

            chunked(down)
            if not backward:
                for i, (a, o) in enumerate(zip((tok, act, gate, up), outs)):
                    pltpu.make_async_copy(a.at[b], o.at[b], save_sem.at[i, b]).start()
            else:
                save = pltpu.make_async_copy(part.at[b], part_out.at[b], save_sem.at[0, b])
                save.start()
                save.wait()
        if backward:
            source = second.at[b] if forward else values

            def back(cols, c):
                da = dot(source[...], w[2, cols], (1,), (1,)) * scale(c)
                gt, u = gate[b, :, cols].astype(F32), up[b, :, cols].astype(F32)
                sig = jax.nn.sigmoid(gt)
                gate[b, :, cols] = (da * u * sig * (1.0 + gt * (1.0 - sig))).astype(BF)
                up[b, :, cols] = (da * gt * sig).astype(BF)

            chunked(back)

            def mix(cols, c):
                total = dot(gate[b], w[0, :, cols], (1,), (0,)) + dot(up[b], w[1, :, cols], (1,), (0,))
                part[b, :, cols] = total.astype(BF)

            chunked(mix)

    def turn(i, carry):
        d = (i + 1) // 2
        b = me + jnp.where(i % 2 == 1, d, -d)

        @pl.when((b >= 0) & (b < n))
        def _():
            @pl.when(i > 0)
            def _():
                move(b, me, 0).wait_recv()

            @pl.when((me < n - 1) & (b <= me))
            def _():
                move(b, me + 1, 0).start()

            @pl.when((me > 0) & (b >= me))
            def _():
                move(b, me - 1, 1).start()

            @pl.when(i == 0)
            def _():
                for k in range(3):
                    pltpu.make_async_copy(w.at[k], w.at[k], w_sem.at[k]).wait()
                for load in loads:
                    load.wait()

            run(b)

            @pl.when((b > me) & (me == 0))
            def _():
                for s in range(SUB):
                    right(b, s).start()

            @pl.when((b < me) & (me == n - 1))
            def _():
                for s in range(SUB):
                    left(b, s).start()

        return carry

    lax.fori_loop(0, 2 * n - 1, turn, 0)

    piece = 2 * small
    slices = width // piece
    total = 3 * slices

    def save_slice(k, slot, out=0):
        unit = 2 * (k % (slices // 2))
        return [
            pltpu.make_async_copy(
                stage.at[slot, pl.ds(v * small, small)], gw_outs[out].at[unit + v, k // slices], save_sem.at[1 + v, slot]
            )
            for v in range(2)
        ]

    def weight_slice(k):
        slot = k % 2
        at = pl.ds(pl.multiple_of(k % slices * piece, HEAD), piece)

        @pl.when(k >= 2)
        def _():
            for copy in save_slice(k - 2, slot):
                copy.wait()

        tokens, grads = (tok, second) if forward else (second, tok)
        for i, (a, v) in enumerate(((gate, tokens), (up, tokens), (act, grads))):
            @pl.when(k // slices == i)
            def _():
                lhs = jnp.concatenate([a[b, :, at] for b in range(n)], 0)
                for c in range(2):
                    cols = pl.ds(c * (width // 2), width // 2)
                    rhs = jnp.concatenate([v[b, :, cols] for b in range(n)], 0)
                    stage[slot, :, cols] = dot(lhs, rhs, (0,), (0,)).astype(BF)

        for out in range(2):
            @pl.when(k % slices // (slices // 2) == out)
            def _():
                for copy in save_slice(k, slot, out):
                    copy.start()

    def add_rows(b, s, slot):
        at = pl.ds(pl.multiple_of(s * sub, sub), sub)
        part[b, at] = (part[b, at].astype(F32) + got[slot, at].astype(F32)).astype(BF)

    count = (n - 1) * SUB

    def relay(t, carry):
        q, s = 1 + t // SUB, t % SUB

        @pl.when((me > 0) & (q > me))
        def _():
            arrived(q, s, q)
            add_rows(q, s, q)
            right(q, s).start()

        @pl.when((me < n - 1) & (n - 1 - q < me))
        def _():
            b = n - 1 - q
            arrived(b, s, b)
            add_rows(b, s, b)
            left(b, s).start()

        if backward:
            def some(k, carry):
                weight_slice(k)
                return carry
            lax.fori_loop(t * total // count, (t + 1) * total // count, some, 0)
        return carry

    lax.fori_loop(0, count, relay, 0)
    y[...] = part[me].astype(F32)

    @pl.when(me > 0)
    def _():
        for s in range(SUB):
            arrived(me, s, me)
        y[...] += got[me].astype(F32)

    @pl.when(me < n - 1)
    def _():
        for s in range(SUB):
            arrived(me, s, n)
        y[...] += got[n].astype(F32)

    if backward:
        for k in (total - 2, total - 1):
            for copy in save_slice(k, k % 2):
                copy.wait()
    for b in range(n):
        if not backward:
            for i, (a, o) in enumerate(zip((tok, act, gate, up), outs)):
                pltpu.make_async_copy(a.at[b], o.at[b], save_sem.at[i, b]).wait()

        @pl.when((me < n - 1) & (b <= me))
        def _():
            move(b, me + 1, 0).wait_send()

        @pl.when((me > 0) & (b >= me))
        def _():
            move(b, me - 1, 1).wait_send()

        @pl.when(b > me)
        def _():
            for s in range(SUB):
                right(b, s).wait_send()

        @pl.when(b < me)
        def _():
            for s in range(SUB):
                left(b, s).wait_send()


def experts(n, forward, backward, x, share, pieces, *more):
    rows, width = x.shape
    small = pieces[0].shape[1]
    hidden = small * 8
    shape = lambda *dims: jax.ShapeDtypeStruct(dims, BF)
    whole, wide = shape(n, rows, width), shape(n, rows, hidden)
    out = [jax.ShapeDtypeStruct((rows, width), F32)]
    out += [] if backward else [whole, wide, wide, wide]
    out += [whole] if forward and backward else []
    out += [shape(4, 3, small, width)] * 2 if backward else []
    room = lambda *dims: pltpu.VMEM(dims, BF)
    scratch = [room(n, rows, width), room(n, rows, width), room(n + 1, rows, width), room(3, hidden, width)]
    scratch += [room(n, rows, hidden)] * 3
    scratch += [room(n, rows, width), room(2, 2 * small, width)] if backward else []
    dma = pltpu.SemaphoreType.DMA
    scratch += [dma((2, n)), dma((n,)), dma((n, SUB)), dma((n + 1, SUB)), dma((3,)), dma((4,)), dma((4, n))]
    vmem, far = pl.BlockSpec(memory_space=pltpu.VMEM), pl.BlockSpec(memory_space=pl.ANY)
    return pl.pallas_call(
        functools.partial(expert_kernel, n, forward, backward),
        out_shape=out,
        in_specs=[vmem, vmem] + [far] * (8 + len(more)),
        out_specs=[vmem] + [far] * (len(out) - 1),
        scratch_shapes=scratch,
        compiler_params=pltpu.CompilerParams(
            collective_id=forward + 2 * backward, has_side_effects=True, vmem_limit_bytes=VMEM_LIMIT
        ),
        cost_estimate=pl.CostEstimate(flops=4 * 10**11, bytes_accessed=10**8, transcendentals=0),
    )(x, share, *pieces, *more)


def turn_head(values, cosine, sine):
    return values * cosine + pltpu.roll(values, HEAD // 2, 1) * sine


def head_group(i):
    own = i // 3
    return jnp.where(lax.axis_index(T) < 2, own, 1 - own)


def lanes(start, size=HEAD):
    return pl.ds(pl.multiple_of(start, HEAD), size)


def loop(count, body):
    def step(i, carry):
        body(i)
        return carry
    lax.fori_loop(0, count, step, 0)


def choose(mine, other, sem, *refs):
    first = lax.axis_index(S) == 0
    for i, (ref, low_first) in enumerate(refs):
        a, b = (mine, other) if low_first else (other, mine)

        @pl.when(first)
        def _():
            pltpu.make_async_copy(a, ref, sem.at[i]).start()

        @pl.when(jnp.logical_not(first))
        def _():
            pltpu.make_async_copy(b, ref, sem.at[i]).start()

    return [pltpu.make_async_copy(mine, ref, sem.at[i]) for i, (ref, _) in enumerate(refs)]


def attend_kernel(
    x, normed, kv, bias, cosine, sine, gain, mine, other, hidden, mixer, queries, flat, logs, wq, wo, sem
):
    pair = 2 * HEAD
    waits = choose(mine, other, sem, (wq, True), (wo, False))
    waits[0].wait()

    def heads(i):
        both = dot(normed[...], wq[lanes(i * pair, pair)], (1,), (1,))
        g = head_group(i)
        keys, values = kv[:, lanes(g * HEAD)], kv[:, lanes((GROUPS + g) * HEAD)]
        for j in range(2):
            at = lanes(i * pair + j * HEAD)
            q = turn_head(both[:, j * HEAD : (j + 1) * HEAD], cosine[...], sine[...]).astype(BF)
            queries[:, at] = q
            scores = dot(q, keys, (1,), (1,)) * HEAD ** (-0.5) + bias[...]
            peak = jnp.max(scores, 1, keepdims=True)
            raised = jnp.exp(scores - peak)
            total = jnp.sum(raised, 1, keepdims=True)
            probs = (raised * (1.0 / total)).astype(BF)
            flat[:, at] = dot(probs, values, (1,), (0,)).astype(BF)
            logs[:, at] = jnp.broadcast_to(peak + jnp.log(total), q.shape)

    loop(HEADS // 2, heads)

    waits[1].wait()

    def out(i):
        cols = lanes(i * pair, pair)
        hidden[:, cols] = x[:, cols].astype(F32) + dot(flat[...], wo[:, cols], (1,), (0,))

    loop(x.shape[1] // pair, out)
    h = hidden[...]
    mixer[...] = (h * inverse_rms(h) * gain[...]).astype(BF)


def attend_back_kernel(
    grad, grad_mixer, hidden, gain, queries, kv, logs, bias, flat, cosine, sine, mine, other,
    grad_hidden, gql, gkv, gwo, grad_gain, gao, ga, acc, wo, sem,
):
    pair = 2 * HEAD
    waits = choose(mine, other, sem, (wo, False))
    scale = HEAD ** (-0.5)
    h = hidden[...]
    r = inverse_rms(h)
    n = h * r
    grad_gain[...] = jnp.sum(grad_mixer[...] * n, 0, keepdims=True)
    m = grad_mixer[...] * gain[...]
    total = grad[...] + r * (m - n * jnp.mean(m * n, -1, keepdims=True))
    grad_hidden[...] = total
    gao[...] = total.astype(BF)
    acc[...] = jnp.zeros_like(acc)
    waits[0].wait()

    def heads(i):
        rows = lanes(i * pair, pair)
        ga[...] = dot(gao[...], wo[rows], (1,), (1,)).astype(BF)
        gwo[rows] = dot(flat[:, rows], gao[...], (0,), (0,)).astype(BF)
        g = head_group(i)
        key_at, value_at = lanes(g * HEAD), lanes((GROUPS + g) * HEAD)
        keys, values = kv[:, key_at], kv[:, value_at]
        for j in range(2):
            at = lanes(i * pair + j * HEAD)
            q, go = queries[:, at], ga[:, j * HEAD : (j + 1) * HEAD]
            scores = dot(q, keys, (1,), (1,)) * scale + bias[...]
            soft = jnp.exp(scores - logs[:, at][:, :1])
            grad_probs = dot(go, values, (1,), (1,))
            inner = jnp.sum(soft * grad_probs, 1, keepdims=True)
            gs = (soft * (grad_probs - inner)).astype(BF)
            gq = dot(gs, keys, (1,), (0,)) * scale
            gql[:, at] = turn_head(gq, cosine[...], -sine[...]).astype(BF)
            acc[:, key_at] += dot(gs, q, (0,), (0,)) * scale
            acc[:, value_at] += dot(soft.astype(BF), go, (0,), (0,))

    loop(HEADS // 2, heads)
    gkv[...] = acc[...].astype(BF)


def local_call(body, flops, out, scratch, *operands):
    return pl.pallas_call(
        body,
        out_shape=[jax.ShapeDtypeStruct(*o) for o in out],
        in_specs=[pl.BlockSpec(memory_space=pltpu.VMEM)] * (len(operands) - 2) + [pl.BlockSpec(memory_space=pl.ANY)] * 2,
        scratch_shapes=[pltpu.VMEM(*s) for s in scratch] + [pltpu.SemaphoreType.DMA((2,))],
        compiler_params=pltpu.CompilerParams(vmem_limit_bytes=VMEM_LIMIT),
        cost_estimate=pl.CostEstimate(flops=flops, bytes_accessed=2 * 10**7, transcendentals=0),
    )(*operands)


def keys_and_values(x, p, c):
    rows = x.shape[0]
    xf = x.astype(F32)
    normed = low(xf * inverse_rms(xf) * p["ga"])
    kv = dot(normed, p["kv"], (1,), (0,)).reshape(rows, 2 * GROUPS, HEAD)
    cosine, sine = c["rope"]
    keys = rotate(kv[:, :GROUPS], cosine[:, None], sine[:, None])
    kv = low(jnp.concatenate([keys, kv[:, GROUPS:]], 1)).reshape(rows, -1)
    return normed, jnp.concatenate(pieces_of(kv))


def attention_forward(x, normed, kv, p, c):
    rows, width = x.shape
    cosine, sine = c["rope"]
    wide = (rows, HEADS * HEAD)
    hidden, mixer, queries, flat, logs = local_call(
        attend_kernel, 10**11, [((rows, width), F32), ((rows, width), BF), (wide, BF), (wide, BF), (wide, F32)],
        [(p["mine"].shape, BF)] * 2,
        x, normed, kv, c["bias"], cosine, sine, p["gm"].reshape(1, -1), p["mine"], p["other"],
    )
    kept = dict(x=x, normed=normed, kv=kv, queries=queries, logs=logs, flat=flat, hidden=hidden)
    return hidden, mixer, kept


def along(values):
    return lax.all_gather(low(values), D, axis=0, tiled=True)


def scatter_along(values):
    return lax.psum_scatter(low(values.reshape(-1, values.shape[-1])), D, scatter_dimension=0, tiled=True)


def weights_of(p):
    f = jnp.stack(p["pieces"])
    return tuple(f[:, i].reshape(-1, f.shape[-1]) for i in range(3))


def share_of(p, hidden):
    return jnp.repeat(p["share"], hidden // 2, axis=1)


def mix_forward(mixer, p, n):
    if n <= SMALL:
        y, tokens, act, gate, up = experts(n, True, False, mixer, p["wide"], p["pieces"])
        return y, dict(tokens=tokens, act=act, gate=gate, up=up)
    wg, wu, wd = weights_of(p)
    tokens = along(mixer)
    gate, up = dot(tokens, wg, (1,), (1,)), dot(tokens, wu, (1,), (1,))
    act = low((jax.nn.silu(gate) * up * share_of(p, wd.shape[0])))
    y = scatter_along(dot(act, wd, (1,), (0,))).astype(F32)
    return y, dict(tokens=tokens, act=act, gate=low(gate), up=low(up))


def mix_backward(grad, k, p, n):
    if n <= SMALL:
        saved = (k["gate"], k["up"], k["act"], k["tokens"])
        return experts(n, False, True, grad, p["wide"], p["pieces"], *saved)
    wg, wu, wd = weights_of(p)
    grads = along(grad)
    da = dot(grads, wd, (1,), (1,)) * share_of(p, wd.shape[0])
    gate, up = k["gate"].astype(F32), k["up"].astype(F32)
    sig = jax.nn.sigmoid(gate)
    dg, du = low((da * up * sig * (1.0 + gate * (1.0 - sig)))), low((da * gate * sig))
    gm = scatter_along(dot(dg, wg, (1,), (0,)) + dot(du, wu, (1,), (0,))).astype(F32)
    flat = lambda v: v.reshape(-1, v.shape[-1])
    pairs = ((dg, k["tokens"]), (du, k["tokens"]), (k["act"], grads))
    gw = [low(dot(flat(u), flat(v), (0,), (0,))) for u, v in pairs]
    gw = jnp.stack([g.reshape(8, -1, g.shape[-1]) for g in gw], 1)
    return gm, gw[:4], gw[4:]


def mix_both(mixer, grad, p, n):
    if n <= SMALL:
        grads = along(grad).reshape(n, *grad.shape)
        gm, part, keep, give = experts(n, True, True, mixer, p["wide"], p["pieces"], grads)
        y = scatter_along(part).astype(F32)
        return y, gm, keep, give
    y, k = mix_forward(mixer, p, n)
    return (y,) + mix_backward(grad, k, p, n)


def attention_backward(grad, grad_mixer, k, p, c, first):
    rows, width = grad.shape
    cosine, sine = c["rope"]
    wide, length = (rows, HEADS * HEAD), c["bias"].shape[1]
    grad_hidden, gql, gkv, gw_out, g_gm = local_call(
        attend_back_kernel, 10**11,
        [((rows, width), F32), (wide, BF), ((length, 2 * GROUPS * HEAD), BF), ((HEADS * HEAD, width), BF), ((1, width), F32)],
        [((rows, width), BF), ((rows, 2 * HEAD), BF), ((length, 2 * GROUPS * HEAD), F32), (p["mine"].shape, BF)],
        grad, grad_mixer, k["hidden"], p["gm"].reshape(1, -1), k["queries"], k["kv"], k["logs"], c["bias"],
        k["flat"], cosine, sine, p["mine"], p["other"],
    )
    gkv = gkv.reshape(4, rows, -1)
    gkv = gkv[0].astype(F32) + sum(hop(gkv[r], r).astype(F32) for r in (1, 2, 3))
    gkv = gkv.reshape(rows, 2 * GROUPS, HEAD)
    cosine, sine = cosine[:, None], sine[:, None]
    gkv = jnp.concatenate([rotate(gkv[:, :GROUPS], cosine, -sine), gkv[:, GROUPS:]], 1)
    gkv = low(gkv).reshape(rows, -1)
    wq = jnp.where(first, p["mine"], p["other"])
    grad_normed = dot(gql, wq, (1,), (0,)) + dot(gkv, p["kv"], (1,), (1,))
    gw_q = low(dot(gql, k["normed"], (0,), (0,)))
    gw_kv = dot(gkv, k["normed"], (0,), (0,))
    more, g_ga = norm_back(grad_normed, k["x"].astype(F32), p["ga"])
    gw_kv = gw_kv.reshape(2, -1, width)
    at = lax.axis_index(T)
    pad = jnp.zeros((63, width), F32)

    def rows_of(main, i, gain):
        less = low(jnp.concatenate([gw_kv[i], gain[None], pad])).reshape(4, -1, width)
        less = jnp.stack([lax.dynamic_index_in_dim(less, at ^ r, 0, False) for r in range(4)])
        return jnp.concatenate([main.reshape(4, -1, width), less], 1)

    q, o = rows_of(gw_q, 0, g_ga), rows_of(gw_out, 1, g_gm[0])
    parts = over_sections(jnp.where(first, q, o), jnp.where(first, o, q))
    return grad_hidden + more, parts


def on_device(
    inputs, cotangent, segments, routes, route_gates, attn_gain, w_query, key_weight,
    value_weight, w_out, mixer_gain, w_gate, w_up, w_down,
):
    section = lax.axis_index(S)
    first = section == 0
    at = lax.axis_index(T)
    rows, width = inputs.shape[1:]
    length = segments.shape[2]
    here = w_gate.shape[1]
    hidden = w_gate.shape[3]
    experts = lax.axis_size(D) * here
    mine = lambda a: lax.dynamic_index_in_dim(a, section, 0, False)
    theirs = lambda a: lax.dynamic_index_in_dim(a, 1 - section, 0, False)
    x0 = mine(inputs)
    grad1 = mine(cotangent)
    segment = mine(segments)[0]

    def halves(own):
        keep, got = mine(own), partner(theirs(own))
        return jnp.where(first, keep, got), jnp.where(first, got, keep)

    named = routes[0][..., None] == jnp.arange(experts, dtype=jnp.int32)
    shares = jnp.sum(jnp.where(named, route_gates[0][..., None], 0.0), 2)
    shares = jnp.stack(halves(shares), 1)

    shares = line_gather(shares)

    def factors(own, l):
        share = own[:, l]
        share = lax.dynamic_slice_in_dim(share, lax.axis_index(D) * here, here, 1)
        share = jnp.where(first, share, share[:, ::-1])
        return jnp.broadcast_to(share.T.reshape(here, -1, rows, 1), (here, share.shape[0] // rows, rows, HEAD)), share

    queries_at = at * rows + jnp.arange(rows)
    keys_at = jnp.concatenate([(at ^ r) * rows + jnp.arange(rows) for r in range(4)])
    key_segment = jnp.concatenate([lax.dynamic_slice_in_dim(segment, (at ^ r) * rows, rows, 0) for r in range(4)])
    allowed = (keys_at[None] <= queries_at[:, None]) & (key_segment[:rows, None] == key_segment[None])
    c = dict(rope=rope_tables(queries_at.astype(F32)), bias=jnp.where(allowed, 0.0, -1e30))

    attn = halves(jnp.stack([w_query[0].T, w_out[0]]))
    g, u = (w[0].transpose(0, 2, 1) for w in (w_gate, w_up))
    ffn = halves(jnp.stack([g, u, w_down[0]], 1))
    kv = both(first, jnp.concatenate([key_weight[0], value_weight[0]], 1))
    ga = both(first, attn_gain)
    gm = both(first, mixer_gain)
    params = []
    last = None
    small = [dict(kv=kv[l], ga=ga[l], gm=gm[l]) for l in range(2)]
    ahead = keys_and_values(x0, small[0], c)
    for l in range(2):
        own = attn[l] if last is None else after(attn[l], last)
        got = pieces_of(own)
        if last is None:
            ffn = after(ffn, got, ahead)
        mine = jnp.concatenate(got)
        wide, share = factors(shares, l)
        got = pieces_of(ffn[l] if last is None else after(ffn[l], last))
        last = got
        params.append(
            dict(
                small[l], mine=mine, other=partner(mine), share=share, wide=wide,
                pieces=got + [partner(v) for v in got],
            )
        )
    n = lax.axis_size(D)
    hidden0, mixer, k0 = attention_forward(x0, *ahead, params[0], c)
    y, kept = mix_forward(mixer, params[0], n)
    y0 = low((hidden0 + y))
    hidden1, mixer, k1 = attention_forward(y0, *keys_and_values(y0, params[1], c), params[1], c)
    y, gm, keep, give = mix_both(mixer, low(grad1), params[1], n)
    y1 = low(hidden1 + y)
    parts = over_sections(keep, give)
    gx1, more = attention_backward(grad1, gm, k1, params[1], c, first)
    gb = low(gx1)
    rows_f = 3 * hidden
    both_parts = [jnp.concatenate([a.reshape(rows_f, width), b]) for a, b in zip(parts, more)]
    gb, both_parts = lax.optimization_barrier((gb, both_parts))
    got = summed(both_parts)
    gm, keep, give = mix_backward(gb, kept, params[0], n)
    gm, got, y1 = lax.optimization_barrier((gm, got, y1))
    f1, s1 = got[:rows_f].reshape(3, hidden, width), lax.psum(got[rows_f:], D)
    parts = over_sections(keep, give)
    part_a = summed([v[:1] for v in parts])
    gx0, more = attention_backward(gb.astype(F32), gm, k0, params[0], c, first)
    s0 = summed(more)
    part_b = summed(after([v[1:] for v in parts], s0))
    f0 = jnp.concatenate([part_a, part_b])
    s0 = lax.psum(after(s0, s1), D)

    outs = jnp.stack(swap(first, y0, y1))
    input_grads = jnp.stack(swap(first, low(gx0), low(gx1))).astype(F32)
    f = jnp.stack(swap(first, f0, f1)).astype(F32)
    zero, one = swap(first, s0, s1)
    high = w_out.shape[1]
    q, o = zero[:high].astype(F32), one[:high].astype(F32)
    less = jnp.stack(pieces_of(jnp.stack([zero[high:], one[high:]])))
    less = jnp.concatenate([lax.dynamic_index_in_dim(less, at ^ i, 0, False) for i in range(4)], 1).astype(F32)
    ka, vm = less[0], less[1]
    few = GROUPS * HEAD
    return (
        outs[None], input_grads[None], ka[few : few + 1], q.T[None], ka[:few].T[None],
        vm[:few].T[None], o[None], vm[few : few + 1], f[:, 0].transpose(0, 2, 1)[None],
        f[:, 1].transpose(0, 2, 1)[None], f[:, 2][None],
    )


def solution(mesh):
    rows, layer, cols = P(None, (D, T), None), P(S, None, (D, T), None), P(S, D, None, T)
    in_specs = (
        rows, rows, P(None, D, None), layer, layer, P(S, None), P(S, None, T), P(S, None, None),
        P(S, None, None), P(S, T, None), P(S, None), cols, cols, P(S, D, T, None),
    )
    out_specs = (
        layer, layer, P(S, None), P(S, None, T), P(S, None, None), P(S, None, None), P(S, T, None),
        P(S, None), cols, cols, P(S, D, T, None),
    )
    return jax.shard_map(on_device, mesh=mesh, in_specs=in_specs, out_specs=out_specs, check_vma=False)
```

```python
import functools
import jax
import jax.numpy as jnp
from jax import lax
from jax.experimental import pallas as pl
from jax.experimental.pallas import tpu as pltpu
from jax.sharding import PartitionSpec as P

S, D, T = "section", "dp", "tensor"
HEADS = 12
GROUPS = 2
HEAD = 128
EPSILON = 1e-06
BF = jnp.bfloat16
F32 = jnp.float32


def dot(a, b, ca, cb):
    return lax.dot_general(a, b, ((ca, cb), ((), ())), preferred_element_type=F32)


def low(values):
    return lax.reduce_precision(values.astype(F32), 8, 7).astype(BF)


def partner(values):
    return lax.ppermute(values, S, [(0, 1), (1, 0)])


def both(first, own):
    other = partner(own)
    return jnp.where(first, own, other), jnp.where(first, other, own)


def swap(first, zero, one):
    keep = jnp.where(first, zero, one)
    got = partner(jnp.where(first, one, zero))
    return jnp.where(first, keep, got), jnp.where(first, got, keep)


def hop(values, bit):
    return lax.ppermute(values, T, [(i, i ^ bit) for i in range(lax.axis_size(T))])


def after(values, *others):
    return lax.optimization_barrier((values, others))[0]


def line_gather(own):
    n, me = lax.axis_size(D), lax.axis_index(D)
    if n != SMALL:
        return lax.all_gather(own, D, axis=0, tiled=True)
    got = [own] + [lax.ppermute(own, D, [(i, i ^ r) for i in range(n)]) for r in range(1, n)]
    got = jnp.stack(got)
    return jnp.concatenate([lax.dynamic_index_in_dim(got, me ^ b, 0, False) for b in range(n)])


def pieces_of(own):
    return [own] + [hop(own, r) for r in (1, 2, 3)]


def add(*values):
    return low(sum(v.astype(F32) for v in values))


def summed(parts):
    return add(parts[0], *(hop(parts[r], r) for r in (1, 2, 3)))


def over_sections(keep, give):
    got = partner(give)
    return [add(keep[r], got[r]) for r in range(4)]


def rope_tables(places):
    half = HEAD // 2
    rates = 10000.0 ** (-jnp.arange(half, dtype=F32) * 2.0 / HEAD)
    angles = places[:, None] * rates[None, :]
    cosine, sine = jnp.cos(angles), jnp.sin(angles)
    return jnp.concatenate([cosine, cosine], 1), jnp.concatenate([-sine, sine], 1)


def rotate(values, cosine, sine):
    half = HEAD // 2
    turned = jnp.concatenate([values[..., half:], values[..., :half]], -1)
    return values * cosine + turned * sine


def inverse_rms(values):
    return lax.rsqrt(jnp.mean(values * values, -1, keepdims=True) + EPSILON)


def norm_back(grad, values, gain):
    r = inverse_rms(values)
    n = values * r
    m = grad * gain
    return r * (m - n * jnp.mean(m * n, -1, keepdims=True)), jnp.sum(grad * n, 0)


MESH = pl.DeviceIdType.MESH
SMALL = 4
SUB = 4
VMEM_LIMIT = 48 * 1024 * 1024


def expert_kernel(n, forward, backward, *refs):
    refs = list(refs)
    take = lambda count: [refs.pop(0) for _ in range(count)]
    x, share = take(2)
    pieces = take(8)
    grads_in = take(1)[0] if forward and backward else None
    saved = take(4) if not forward else None
    y = take(1)[0]
    outs = take(4) if not backward else None
    part_out = take(1)[0] if forward and backward else None
    gw_outs = take(2) if backward else None
    tok, part, got, w, gate, up, act = take(7)
    second = take(1)[0] if backward else None
    stage = take(1)[0] if backward else None
    tok_send, tok_recv, part_send, part_recv, w_sem, io_sem, save_sem = refs
    rows, width = x.shape
    sub = rows // SUB
    me = lax.axis_index(D)

    small = w.shape[1] // 8
    for i in range(3):
        for k, one in enumerate(pieces):
            rows_at = pl.ds(one.shape[0] - (3 - i) * small, small)
            pltpu.make_async_copy(one.at[rows_at], w.at[i, pl.ds(k * small, small)], w_sem.at[i]).start()
    loads = []
    if saved is not None:
        loads = [pltpu.make_async_copy(a, o, io_sem.at[i]) for i, (a, o) in enumerate(zip(saved, (gate, up, act, second)))]
    elif backward:
        loads = [pltpu.make_async_copy(grads_in, second, io_sem.at[0])]
    for load in loads:
        load.start()
    barrier = pltpu.get_barrier_semaphore()
    for step in (-1, 1):
        @pl.when((me + step >= 0) & (me + step < n))
        def _():
            pl.semaphore_signal(barrier, inc=1, device_id={D: me + step}, device_id_type=MESH)
    tok[me] = x[...]
    pl.semaphore_wait(barrier, jnp.where((me == 0) | (me == n - 1), 1, 2))

    def move(b, to, side):
        return pltpu.make_async_remote_copy(
            src_ref=tok.at[b], dst_ref=tok.at[b], send_sem=tok_send.at[side, b], recv_sem=tok_recv.at[b],
            device_id={D: to}, device_id_type=MESH,
        )

    def pass_sum(b, s, to, slot):
        at = pl.ds(pl.multiple_of(s * sub, sub), sub)
        return pltpu.make_async_remote_copy(
            src_ref=part.at[b, at], dst_ref=got.at[slot, at], send_sem=part_send.at[b, s],
            recv_sem=part_recv.at[slot, s], device_id={D: to}, device_id_type=MESH,
        )

    def right(b, s):
        return pass_sum(b, s, me + 1, b)

    def left(b, s):
        return pass_sum(b, s, me - 1, jnp.where(b == me - 1, n, b))

    def arrived(b, s, slot):
        pass_sum(b, s, me, slot).wait_recv()

    chunk = 256
    steps = width // chunk

    def chunked(body):
        def step(c, carry):
            body(pl.ds(pl.multiple_of(c * chunk, chunk), chunk), c)
            return carry
        lax.fori_loop(0, steps, step, 0)

    def run(b):
        values = tok.at[b]

        def scale(c):
            s = share[c * 2 // steps, b]
            return jnp.concatenate([s, s], 1)

        if forward:
            def ahead(cols, c):
                gt = dot(values[...], w[0, cols], (1,), (1,))
                u = dot(values[...], w[1, cols], (1,), (1,))
                gate[b, :, cols] = gt.astype(BF)
                up[b, :, cols] = u.astype(BF)
                act[b, :, cols] = (gt * jax.nn.sigmoid(gt) * u * scale(c)).astype(BF)

            chunked(ahead)

            def down(cols, c):
                part[b, :, cols] = dot(act[b], w[2, :, cols], (1,), (0,)).astype(BF)

            chunked(down)
            if not backward:
                for i, (a, o) in enumerate(zip((tok, act, gate, up), outs)):
                    pltpu.make_async_copy(a.at[b], o.at[b], save_sem.at[i, b]).start()
            else:
                save = pltpu.make_async_copy(part.at[b], part_out.at[b], save_sem.at[0, b])
                save.start()
                save.wait()
        if backward:
            source = second.at[b] if forward else values

            def back(cols, c):
                da = dot(source[...], w[2, cols], (1,), (1,)) * scale(c)
                gt, u = gate[b, :, cols].astype(F32), up[b, :, cols].astype(F32)
                sig = jax.nn.sigmoid(gt)
                gate[b, :, cols] = (da * u * sig * (1.0 + gt * (1.0 - sig))).astype(BF)
                up[b, :, cols] = (da * gt * sig).astype(BF)

            chunked(back)

            def mix(cols, c):
                total = dot(gate[b], w[0, :, cols], (1,), (0,)) + dot(up[b], w[1, :, cols], (1,), (0,))
                part[b, :, cols] = total.astype(BF)

            chunked(mix)

    def turn(i, carry):
        d = (i + 1) // 2
        b = me + jnp.where(i % 2 == 1, d, -d)

        @pl.when((b >= 0) & (b < n))
        def _():
            @pl.when(i > 0)
            def _():
                move(b, me, 0).wait_recv()

            @pl.when((me < n - 1) & (b <= me))
            def _():
                move(b, me + 1, 0).start()

            @pl.when((me > 0) & (b >= me))
            def _():
                move(b, me - 1, 1).start()

            @pl.when(i == 0)
            def _():
                for k in range(3):
                    pltpu.make_async_copy(w.at[k], w.at[k], w_sem.at[k]).wait()
                for load in loads:
                    load.wait()

            run(b)

            @pl.when((b > me) & (me == 0))
            def _():
                for s in range(SUB):
                    right(b, s).start()

            @pl.when((b < me) & (me == n - 1))
            def _():
                for s in range(SUB):
                    left(b, s).start()

        return carry

    lax.fori_loop(0, 2 * n - 1, turn, 0)

    piece = 2 * small
    slices = width // piece
    total = 3 * slices

    def save_slice(k, slot, out=0):
        unit = 2 * (k % (slices // 2))
        return [
            pltpu.make_async_copy(
                stage.at[slot, pl.ds(v * small, small)], gw_outs[out].at[unit + v, k // slices], save_sem.at[1 + v, slot]
            )
            for v in range(2)
        ]

    def weight_slice(k):
        slot = k % 2
        at = pl.ds(pl.multiple_of(k % slices * piece, HEAD), piece)

        @pl.when(k >= 2)
        def _():
            for copy in save_slice(k - 2, slot):
                copy.wait()

        tokens, grads = (tok, second) if forward else (second, tok)
        for i, (a, v) in enumerate(((gate, tokens), (up, tokens), (act, grads))):
            @pl.when(k // slices == i)
            def _():
                lhs = jnp.concatenate([a[b, :, at] for b in range(n)], 0)
                for c in range(2):
                    cols = pl.ds(c * (width // 2), width // 2)
                    rhs = jnp.concatenate([v[b, :, cols] for b in range(n)], 0)
                    stage[slot, :, cols] = dot(lhs, rhs, (0,), (0,)).astype(BF)

        for out in range(2):
            @pl.when(k % slices // (slices // 2) == out)
            def _():
                for copy in save_slice(k, slot, out):
                    copy.start()

    def add_rows(b, s, slot):
        at = pl.ds(pl.multiple_of(s * sub, sub), sub)
        part[b, at] = (part[b, at].astype(F32) + got[slot, at].astype(F32)).astype(BF)

    count = (n - 1) * SUB

    def relay(t, carry):
        q, s = 1 + t // SUB, t % SUB

        @pl.when((me > 0) & (q > me))
        def _():
            arrived(q, s, q)
            add_rows(q, s, q)
            right(q, s).start()

        @pl.when((me < n - 1) & (n - 1 - q < me))
        def _():
            b = n - 1 - q
            arrived(b, s, b)
            add_rows(b, s, b)
            left(b, s).start()

        if backward:
            def some(k, carry):
                weight_slice(k)
                return carry
            lax.fori_loop(t * total // count, (t + 1) * total // count, some, 0)
        return carry

    lax.fori_loop(0, count, relay, 0)
    y[...] = part[me].astype(F32)

    @pl.when(me > 0)
    def _():
        for s in range(SUB):
            arrived(me, s, me)
        y[...] += got[me].astype(F32)

    @pl.when(me < n - 1)
    def _():
        for s in range(SUB):
            arrived(me, s, n)
        y[...] += got[n].astype(F32)

    if backward:
        for k in (total - 2, total - 1):
            for copy in save_slice(k, k % 2):
                copy.wait()
    for b in range(n):
        if not backward:
            for i, (a, o) in enumerate(zip((tok, act, gate, up), outs)):
                pltpu.make_async_copy(a.at[b], o.at[b], save_sem.at[i, b]).wait()

        @pl.when((me < n - 1) & (b <= me))
        def _():
            move(b, me + 1, 0).wait_send()

        @pl.when((me > 0) & (b >= me))
        def _():
            move(b, me - 1, 1).wait_send()

        @pl.when(b > me)
        def _():
            for s in range(SUB):
                right(b, s).wait_send()

        @pl.when(b < me)
        def _():
            for s in range(SUB):
                left(b, s).wait_send()


def experts(n, forward, backward, x, share, small, pieces, *more):
    rows, width = x.shape
    hidden = small * 8
    shape = lambda *dims: jax.ShapeDtypeStruct(dims, BF)
    whole, wide = shape(n, rows, width), shape(n, rows, hidden)
    out = [jax.ShapeDtypeStruct((rows, width), F32)]
    out += [] if backward else [whole, wide, wide, wide]
    out += [whole] if forward and backward else []
    out += [shape(4, 3, small, width)] * 2 if backward else []
    room = lambda *dims: pltpu.VMEM(dims, BF)
    scratch = [room(n, rows, width), room(n, rows, width), room(n + 1, rows, width), room(3, hidden, width)]
    scratch += [room(n, rows, hidden)] * 3
    scratch += [room(n, rows, width), room(2, 2 * small, width)] if backward else []
    dma = pltpu.SemaphoreType.DMA
    scratch += [dma((2, n)), dma((n,)), dma((n, SUB)), dma((n + 1, SUB)), dma((3,)), dma((4,)), dma((4, n))]
    vmem, far = pl.BlockSpec(memory_space=pltpu.VMEM), pl.BlockSpec(memory_space=pl.ANY)
    return pl.pallas_call(
        functools.partial(expert_kernel, n, forward, backward),
        out_shape=out,
        in_specs=[vmem, vmem] + [far] * (8 + len(more)),
        out_specs=[vmem] + [far] * (len(out) - 1),
        scratch_shapes=scratch,
        compiler_params=pltpu.CompilerParams(
            collective_id=forward + 2 * backward, has_side_effects=True, vmem_limit_bytes=VMEM_LIMIT
        ),
        cost_estimate=pl.CostEstimate(flops=4 * 10**11, bytes_accessed=10**8, transcendentals=0),
    )(x, share, *pieces, *more)


def turn_head(values, cosine, sine):
    return values * cosine + pltpu.roll(values, HEAD // 2, 1) * sine


def head_group(i):
    own = i // 3
    return jnp.where(lax.axis_index(T) < 2, own, 1 - own)


def lanes(start, size=HEAD):
    return pl.ds(pl.multiple_of(start, HEAD), size)


def loop(count, body):
    def step(i, carry):
        body(i)
        return carry
    lax.fori_loop(0, count, step, 0)


def choose(mine, other, sem, *refs):
    first = lax.axis_index(S) == 0
    for i, (ref, low_first) in enumerate(refs):
        a, b = (mine, other) if low_first else (other, mine)

        @pl.when(first)
        def _():
            pltpu.make_async_copy(a, ref, sem.at[i]).start()

        @pl.when(jnp.logical_not(first))
        def _():
            pltpu.make_async_copy(b, ref, sem.at[i]).start()

    return [pltpu.make_async_copy(mine, ref, sem.at[i]) for i, (ref, _) in enumerate(refs)]


def attend_kernel(
    x, normed, kv, bias, cosine, sine, gain, mine, other, hidden, mixer, queries, flat, logs, wq, wo, sem
):
    pair = 2 * HEAD
    waits = choose(mine, other, sem, (wq, True), (wo, False))
    waits[0].wait()

    def heads(i):
        both = dot(normed[...], wq[lanes(i * pair, pair)], (1,), (1,))
        g = head_group(i)
        keys, values = kv[:, lanes(g * HEAD)], kv[:, lanes((GROUPS + g) * HEAD)]
        for j in range(2):
            at = lanes(i * pair + j * HEAD)
            q = turn_head(both[:, j * HEAD : (j + 1) * HEAD], cosine[...], sine[...]).astype(BF)
            queries[:, at] = q
            scores = dot(q, keys, (1,), (1,)) * HEAD ** (-0.5) + bias[...]
            peak = jnp.max(scores, 1, keepdims=True)
            raised = jnp.exp(scores - peak)
            total = jnp.sum(raised, 1, keepdims=True)
            probs = (raised * (1.0 / total)).astype(BF)
            flat[:, at] = dot(probs, values, (1,), (0,)).astype(BF)
            logs[:, at] = jnp.broadcast_to(peak + jnp.log(total), q.shape)

    loop(HEADS // 2, heads)

    waits[1].wait()

    def out(i):
        cols = lanes(i * pair, pair)
        hidden[:, cols] = x[:, cols].astype(F32) + dot(flat[...], wo[:, cols], (1,), (0,))

    loop(x.shape[1] // pair, out)
    h = hidden[...]
    mixer[...] = (h * inverse_rms(h) * gain[...]).astype(BF)


def attend_back_kernel(
    grad, grad_mixer, hidden, gain, queries, kv, logs, bias, flat, cosine, sine, mine, other,
    grad_hidden, gql, gkv, gwo, grad_gain, gao, ga, acc, wo, sem,
):
    pair = 2 * HEAD
    waits = choose(mine, other, sem, (wo, False))
    scale = HEAD ** (-0.5)
    h = hidden[...]
    r = inverse_rms(h)
    n = h * r
    grad_gain[...] = jnp.sum(grad_mixer[...] * n, 0, keepdims=True)
    m = grad_mixer[...] * gain[...]
    total = grad[...] + r * (m - n * jnp.mean(m * n, -1, keepdims=True))
    grad_hidden[...] = total
    gao[...] = total.astype(BF)
    acc[...] = jnp.zeros_like(acc)
    waits[0].wait()

    def heads(i):
        rows = lanes(i * pair, pair)
        ga[...] = dot(gao[...], wo[rows], (1,), (1,)).astype(BF)
        gwo[rows] = dot(flat[:, rows], gao[...], (0,), (0,)).astype(BF)
        g = head_group(i)
        key_at, value_at = lanes(g * HEAD), lanes((GROUPS + g) * HEAD)
        keys, values = kv[:, key_at], kv[:, value_at]
        for j in range(2):
            at = lanes(i * pair + j * HEAD)
            q, go = queries[:, at], ga[:, j * HEAD : (j + 1) * HEAD]
            scores = dot(q, keys, (1,), (1,)) * scale + bias[...]
            soft = jnp.exp(scores - logs[:, at][:, :1])
            grad_probs = dot(go, values, (1,), (1,))
            inner = jnp.sum(soft * grad_probs, 1, keepdims=True)
            gs = (soft * (grad_probs - inner)).astype(BF)
            gq = dot(gs, keys, (1,), (0,)) * scale
            gql[:, at] = turn_head(gq, cosine[...], -sine[...]).astype(BF)
            acc[:, key_at] += dot(gs, q, (0,), (0,)) * scale
            acc[:, value_at] += dot(soft.astype(BF), go, (0,), (0,))

    loop(HEADS // 2, heads)
    gkv[...] = acc[...].astype(BF)


def local_call(body, flops, out, scratch, *operands):
    return pl.pallas_call(
        body,
        out_shape=[jax.ShapeDtypeStruct(*o) for o in out],
        in_specs=[pl.BlockSpec(memory_space=pltpu.VMEM)] * (len(operands) - 2) + [pl.BlockSpec(memory_space=pl.ANY)] * 2,
        scratch_shapes=[pltpu.VMEM(*s) for s in scratch] + [pltpu.SemaphoreType.DMA((2,))],
        compiler_params=pltpu.CompilerParams(vmem_limit_bytes=VMEM_LIMIT),
        cost_estimate=pl.CostEstimate(flops=flops, bytes_accessed=2 * 10**7, transcendentals=0),
    )(*operands)


def keys_and_values(x, p, c, *before):
    rows = x.shape[0]
    xf = x.astype(F32)
    normed = low(xf * inverse_rms(xf) * p["ga"])
    kv = dot(normed, p["kv"], (1,), (0,)).reshape(rows, 2 * GROUPS, HEAD)
    cosine, sine = c["rope"]
    keys = rotate(kv[:, :GROUPS], cosine[:, None], sine[:, None])
    kv = low(jnp.concatenate([keys, kv[:, GROUPS:]], 1)).reshape(rows, -1)
    return normed, jnp.concatenate(pieces_of(after(kv, *before)))


def attention_forward(x, normed, kv, p, c):
    rows, width = x.shape
    cosine, sine = c["rope"]
    wide = (rows, HEADS * HEAD)
    hidden, mixer, queries, flat, logs = local_call(
        attend_kernel, 10**11, [((rows, width), F32), ((rows, width), BF), (wide, BF), (wide, BF), (wide, F32)],
        [(p["mine"].shape, BF)] * 2,
        x, normed, kv, c["bias"], cosine, sine, p["gm"].reshape(1, -1), p["mine"], p["other"],
    )
    kept = dict(x=x, normed=normed, kv=kv, queries=queries, logs=logs, flat=flat, hidden=hidden)
    return hidden, mixer, kept


def along(values):
    return lax.all_gather(low(values), D, axis=0, tiled=True)


def scatter_along(values):
    return lax.psum_scatter(low(values.reshape(-1, values.shape[-1])), D, scatter_dimension=0, tiled=True)


def weights_of(p):
    f = jnp.stack([v[-3 * p["unit"] :].reshape(3, p["unit"], -1) for v in p["pieces"]])
    return tuple(f[:, i].reshape(-1, f.shape[-1]) for i in range(3))


def share_of(p, hidden):
    return jnp.repeat(p["share"], hidden // 2, axis=1)


def mix_forward(mixer, p, n):
    if n <= SMALL:
        y, tokens, act, gate, up = experts(n, True, False, mixer, p["wide"], p["unit"], p["pieces"])
        return y, dict(tokens=tokens, act=act, gate=gate, up=up)
    wg, wu, wd = weights_of(p)
    tokens = along(mixer)
    gate, up = dot(tokens, wg, (1,), (1,)), dot(tokens, wu, (1,), (1,))
    act = low((jax.nn.silu(gate) * up * share_of(p, wd.shape[0])))
    y = scatter_along(dot(act, wd, (1,), (0,))).astype(F32)
    return y, dict(tokens=tokens, act=act, gate=low(gate), up=low(up))


def mix_backward(grad, k, p, n):
    if n <= SMALL:
        saved = (k["gate"], k["up"], k["act"], k["tokens"])
        return experts(n, False, True, grad, p["wide"], p["unit"], p["pieces"], *saved)
    wg, wu, wd = weights_of(p)
    grads = along(grad)
    da = dot(grads, wd, (1,), (1,)) * share_of(p, wd.shape[0])
    gate, up = k["gate"].astype(F32), k["up"].astype(F32)
    sig = jax.nn.sigmoid(gate)
    dg, du = low((da * up * sig * (1.0 + gate * (1.0 - sig)))), low((da * gate * sig))
    gm = scatter_along(dot(dg, wg, (1,), (0,)) + dot(du, wu, (1,), (0,))).astype(F32)
    flat = lambda v: v.reshape(-1, v.shape[-1])
    pairs = ((dg, k["tokens"]), (du, k["tokens"]), (k["act"], grads))
    gw = [low(dot(flat(u), flat(v), (0,), (0,))) for u, v in pairs]
    gw = jnp.stack([g.reshape(8, -1, g.shape[-1]) for g in gw], 1)
    return gm, gw[:4], gw[4:]


def mix_both(mixer, grad, p, n, grads):
    if n <= SMALL:
        grads = grads.reshape(n, *grad.shape)
        gm, part, keep, give = experts(n, True, True, mixer, p["wide"], p["unit"], p["pieces"], grads)
        return part, gm, keep, give
    y, k = mix_forward(mixer, p, n)
    return (y,) + mix_backward(grad, k, p, n)


def attention_backward(grad, grad_mixer, k, p, c, first, early):
    rows, width = grad.shape
    cosine, sine = c["rope"]
    wide, length = (rows, HEADS * HEAD), c["bias"].shape[1]
    grad_hidden, gql, gkv, gw_out, g_gm = local_call(
        attend_back_kernel, 10**11,
        [((rows, width), F32), (wide, BF), ((length, 2 * GROUPS * HEAD), BF), ((HEADS * HEAD, width), BF), ((1, width), F32)],
        [((rows, width), BF), ((rows, 2 * HEAD), BF), ((length, 2 * GROUPS * HEAD), F32), (p["mine"].shape, BF)],
        grad, grad_mixer, k["hidden"], p["gm"].reshape(1, -1), k["queries"], k["kv"], k["logs"], c["bias"],
        k["flat"], cosine, sine, p["mine"], p["other"],
    )
    gkv, early = lax.optimization_barrier((gkv.reshape(4, rows, -1), early))
    part = summed([v[:1] for v in early]) if early else ()
    gkv = gkv[0].astype(F32) + sum(hop(gkv[r], r).astype(F32) for r in (1, 2, 3))
    gkv, part = lax.optimization_barrier((gkv, part))
    gkv = gkv.reshape(rows, 2 * GROUPS, HEAD)
    cosine, sine = cosine[:, None], sine[:, None]
    gkv = jnp.concatenate([rotate(gkv[:, :GROUPS], cosine, -sine), gkv[:, GROUPS:]], 1)
    gkv = low(gkv).reshape(rows, -1)
    wq = jnp.where(first, p["mine"], p["other"])
    grad_normed = dot(gql, wq, (1,), (0,)) + dot(gkv, p["kv"], (1,), (1,))
    gw_q = low(dot(gql, k["normed"], (0,), (0,)))
    gw_kv = dot(gkv, k["normed"], (0,), (0,))
    more, g_ga = norm_back(grad_normed, k["x"].astype(F32), p["ga"])
    gw_kv = gw_kv.reshape(2, -1, width)
    at = lax.axis_index(T)
    pad = jnp.zeros((63, width), F32)

    def rows_of(main, i, gain):
        less = low(jnp.concatenate([gw_kv[i], gain[None], pad])).reshape(4, -1, width)
        less = jnp.stack([lax.dynamic_index_in_dim(less, at ^ r, 0, False) for r in range(4)])
        return jnp.concatenate([main.reshape(4, -1, width), less], 1)

    q, o = rows_of(gw_q, 0, g_ga), rows_of(gw_out, 1, g_gm[0])
    parts = over_sections(jnp.where(first, q, o), jnp.where(first, o, q))
    return grad_hidden + more, parts, part, early


def on_device(
    inputs, cotangent, segments, routes, route_gates, attn_gain, w_query, key_weight,
    value_weight, w_out, mixer_gain, w_gate, w_up, w_down,
):
    section = lax.axis_index(S)
    first = section == 0
    at = lax.axis_index(T)
    rows, width = inputs.shape[1:]
    length = segments.shape[2]
    here = w_gate.shape[1]
    hidden = w_gate.shape[3]
    experts = lax.axis_size(D) * here
    mine = lambda a: lax.dynamic_index_in_dim(a, section, 0, False)
    theirs = lambda a: lax.dynamic_index_in_dim(a, 1 - section, 0, False)
    x0 = mine(inputs)
    grad1 = mine(cotangent)
    segment = mine(segments)[0]

    def halves(own):
        keep, got = mine(own), partner(theirs(own))
        return jnp.where(first, keep, got), jnp.where(first, got, keep)

    named = routes[0][..., None] == jnp.arange(experts, dtype=jnp.int32)
    shares = jnp.sum(jnp.where(named, route_gates[0][..., None], 0.0), 2)
    shares = jnp.stack(halves(shares), 1)

    shares = line_gather(shares)

    def factors(own, l):
        share = own[:, l]
        share = lax.dynamic_slice_in_dim(share, lax.axis_index(D) * here, here, 1)
        share = jnp.stack([jnp.where(first, share[:, i], share[:, 1 - i]) for i in range(2)], 1)
        return jnp.broadcast_to(share.T.reshape(here, -1, rows, 1), (here, share.shape[0] // rows, rows, HEAD)), share

    queries_at = at * rows + jnp.arange(rows)
    keys_at = jnp.concatenate([(at ^ r) * rows + jnp.arange(rows) for r in range(4)])
    key_segment = jnp.concatenate([lax.dynamic_slice_in_dim(segment, (at ^ r) * rows, rows, 0) for r in range(4)])
    allowed = (keys_at[None] <= queries_at[:, None]) & (key_segment[:rows, None] == key_segment[None])
    c = dict(rope=rope_tables(queries_at.astype(F32)), bias=jnp.where(allowed, 0.0, -1e30))

    attn = halves(jnp.stack([w_query[0].T, w_out[0]]))
    g, u = (w[0].transpose(0, 2, 1) for w in (w_gate, w_up))
    ffn = halves(jnp.stack([g, u, w_down[0]], 1))
    kv = both(first, jnp.concatenate([key_weight[0], value_weight[0]], 1))
    ga = both(first, attn_gain)
    gm = both(first, mixer_gain)
    n = lax.axis_size(D)
    small = [dict(kv=kv[l], ga=ga[l], gm=gm[l], unit=hidden) for l in range(2)]
    for l, one in enumerate(small):
        one["wide"], one["share"] = factors(shares, l)
    grads = along(low(grad1)) if n <= SMALL else low(grad1)
    ffn = [v.reshape(-1, width) for v in ffn]
    high = w_out.shape[1]

    ahead = keys_and_values(x0, small[0], c)
    got = pieces_of(attn[0])
    late = after(ffn[0], got, ahead, grads)
    mine = jnp.concatenate(got)
    small[0].update(mine=mine, other=partner(mine))
    hidden0, mixer, k0 = attention_forward(x0, *ahead, small[0], c)
    got = pieces_of(late)
    crossed = after(got, mixer)
    small[0].update(pieces=got + [partner(v) for v in crossed])
    more = pieces_of(after(jnp.concatenate([attn[1], ffn[1]]), got))
    y, kept = mix_forward(mixer, small[0], n)
    y0 = low((hidden0 + y))
    other = [partner(v) for v in after(more, y)]
    small[1].update(
        mine=jnp.concatenate([v[:high] for v in more]), other=jnp.concatenate([v[:high] for v in other]),
        pieces=more + other,
    )
    hidden1, mixer, k1 = attention_forward(y0, *keys_and_values(y0, small[1], c, other), small[1], c)
    y, gm, keep, give = mix_both(mixer, low(grad1), small[1], n, grads)
    parts = over_sections(keep, give)
    gx1, more, _, _ = attention_backward(grad1, gm, k1, small[1], c, first, [])
    gb = low(gx1)
    rows_f = 3 * hidden
    both_parts = [jnp.concatenate([a.reshape(rows_f, width), b]) for a, b in zip(parts, more)]
    gb, both_parts = lax.optimization_barrier((gb, both_parts))
    got = summed(both_parts)
    gm, keep, give = mix_backward(gb, kept, small[0], n)
    gm, got, y = lax.optimization_barrier((gm, got, y))
    y1 = low(hidden1 + (scatter_along(y).astype(F32) if n <= SMALL else y))
    f1, s1 = got[:rows_f].reshape(3, hidden, width), lax.psum(got[rows_f:], D)
    parts = over_sections(keep, give)
    gx0, more, part_a, parts = attention_backward(gb.astype(F32), gm, k0, small[0], c, first, parts)
    s0 = summed(more)
    part_b = summed(after([v[1:] for v in parts], s0))
    f0 = jnp.concatenate([part_a, part_b])
    s0 = lax.psum(after(s0, s1, y1), D)

    outs = jnp.stack(swap(first, y0, y1))
    input_grads = jnp.stack(swap(first, low(gx0), low(gx1))).astype(F32)
    f = jnp.stack(swap(first, f0, f1)).astype(F32)
    zero, one = swap(first, s0, s1)
    q, o = zero[:high].astype(F32), one[:high].astype(F32)
    less = jnp.stack(pieces_of(jnp.stack([zero[high:], one[high:]])))
    less = jnp.concatenate([lax.dynamic_index_in_dim(less, at ^ i, 0, False) for i in range(4)], 1).astype(F32)
    ka, vm = less[0], less[1]
    few = GROUPS * HEAD
    return (
        outs[None], input_grads[None], ka[few : few + 1], q.T[None], ka[:few].T[None],
        vm[:few].T[None], o[None], vm[few : few + 1], f[:, 0].transpose(0, 2, 1)[None],
        f[:, 1].transpose(0, 2, 1)[None], f[:, 2][None],
    )


def solution(mesh):
    rows, layer, cols = P(None, (D, T), None), P(S, None, (D, T), None), P(S, D, None, T)
    in_specs = (
        rows, rows, P(None, D, None), layer, layer, P(S, None), P(S, None, T), P(S, None, None),
        P(S, None, None), P(S, T, None), P(S, None), cols, cols, P(S, D, T, None),
    )
    out_specs = (
        layer, layer, P(S, None), P(S, None, T), P(S, None, None), P(S, None, None), P(S, T, None),
        P(S, None), cols, cols, P(S, D, T, None),
    )
    return jax.shard_map(on_device, mesh=mesh, in_specs=in_specs, out_specs=out_specs, check_vma=False)
```

```python
import functools
import jax
import jax.numpy as jnp
from jax import lax
from jax.experimental import pallas as pl
from jax.experimental.pallas import tpu as pltpu
from jax.sharding import PartitionSpec as P

S, D, T = "section", "dp", "tensor"
HEADS = 12
GROUPS = 2
HEAD = 128
EPSILON = 1e-06
BF = jnp.bfloat16
F32 = jnp.float32


def dot(a, b, ca, cb):
    return lax.dot_general(a, b, ((ca, cb), ((), ())), preferred_element_type=F32)


def low(values):
    return lax.reduce_precision(values.astype(F32), 8, 7).astype(BF)


def partner(values):
    return lax.ppermute(values, S, [(0, 1), (1, 0)])


def both(first, own):
    other = partner(own)
    return jnp.where(first, own, other), jnp.where(first, other, own)


def swap(first, zero, one):
    keep = jnp.where(first, zero, one)
    got = partner(jnp.where(first, one, zero))
    return jnp.where(first, keep, got), jnp.where(first, got, keep)


def hop(values, bit):
    return lax.ppermute(values, T, [(i, i ^ bit) for i in range(lax.axis_size(T))])


def after(values, *others):
    return lax.optimization_barrier((values, others))[0]


def line_gather(own):
    n, me = lax.axis_size(D), lax.axis_index(D)
    if n != SMALL:
        return lax.all_gather(own, D, axis=0, tiled=True)
    got = [own] + [lax.ppermute(own, D, [(i, i ^ r) for i in range(n)]) for r in range(1, n)]
    got = jnp.stack(got)
    return jnp.concatenate([lax.dynamic_index_in_dim(got, me ^ b, 0, False) for b in range(n)])


def pieces_of(own):
    return [own] + [hop(own, r) for r in (1, 2, 3)]


def add(*values):
    return low(sum(v.astype(F32) for v in values))


def summed(parts):
    return add(parts[0], *(hop(parts[r], r) for r in (1, 2, 3)))


def over_sections(keep, give):
    got = partner(give)
    return [add(keep[r], got[r]) for r in range(4)]


def rope_tables(places):
    half = HEAD // 2
    rates = 10000.0 ** (-jnp.arange(half, dtype=F32) * 2.0 / HEAD)
    angles = places[:, None] * rates[None, :]
    cosine, sine = jnp.cos(angles), jnp.sin(angles)
    return jnp.concatenate([cosine, cosine], 1), jnp.concatenate([-sine, sine], 1)


def rotate(values, cosine, sine):
    half = HEAD // 2
    turned = jnp.concatenate([values[..., half:], values[..., :half]], -1)
    return values * cosine + turned * sine


def inverse_rms(values):
    return lax.rsqrt(jnp.mean(values * values, -1, keepdims=True) + EPSILON)


def norm_back(grad, values, gain):
    r = inverse_rms(values)
    n = values * r
    m = grad * gain
    return r * (m - n * jnp.mean(m * n, -1, keepdims=True)), jnp.sum(grad * n, 0)


MESH = pl.DeviceIdType.MESH
SMALL = 4
SUB = 4
VMEM_LIMIT = 48 * 1024 * 1024


def expert_kernel(n, forward, backward, *refs):
    refs = list(refs)
    take = lambda count: [refs.pop(0) for _ in range(count)]
    x, share = take(2)
    pieces = take(8)
    grads_in = take(1)[0] if forward and backward else None
    saved = take(4) if not forward else None
    y = take(1)[0]
    outs = take(4) if not backward else None
    part_out = take(1)[0] if forward and backward else None
    gw_outs = take(2) if backward else None
    tok, part, got, w, gate, up, act = take(7)
    second = take(1)[0] if backward else None
    stage = take(1)[0] if backward else None
    tok_send, tok_recv, part_send, part_recv, w_sem, io_sem, save_sem = refs
    rows, width = x.shape
    sub = rows // SUB
    me = lax.axis_index(D)

    small = w.shape[1] // 8
    for i in range(3):
        for k, one in enumerate(pieces):
            rows_at = pl.ds(one.shape[0] - (3 - i) * small, small)
            pltpu.make_async_copy(one.at[rows_at], w.at[i, pl.ds(k * small, small)], w_sem.at[i]).start()
    loads = []
    if saved is not None:
        loads = [pltpu.make_async_copy(a, o, io_sem.at[i]) for i, (a, o) in enumerate(zip(saved, (gate, up, act, second)))]
    elif backward:
        loads = [pltpu.make_async_copy(grads_in, second, io_sem.at[0])]
    for load in loads:
        load.start()
    barrier = pltpu.get_barrier_semaphore()
    for step in (-1, 1):
        @pl.when((me + step >= 0) & (me + step < n))
        def _():
            pl.semaphore_signal(barrier, inc=1, device_id={D: me + step}, device_id_type=MESH)
    tok[me] = x[...]
    pl.semaphore_wait(barrier, jnp.where((me == 0) | (me == n - 1), 1, 2))

    def move(b, to, side):
        return pltpu.make_async_remote_copy(
            src_ref=tok.at[b], dst_ref=tok.at[b], send_sem=tok_send.at[side, b], recv_sem=tok_recv.at[b],
            device_id={D: to}, device_id_type=MESH,
        )

    def pass_sum(b, s, to, slot):
        at = pl.ds(pl.multiple_of(s * sub, sub), sub)
        return pltpu.make_async_remote_copy(
            src_ref=part.at[b, at], dst_ref=got.at[slot, at], send_sem=part_send.at[b, s],
            recv_sem=part_recv.at[slot, s], device_id={D: to}, device_id_type=MESH,
        )

    def right(b, s):
        return pass_sum(b, s, me + 1, b)

    def left(b, s):
        return pass_sum(b, s, me - 1, jnp.where(b == me - 1, n, b))

    def arrived(b, s, slot):
        pass_sum(b, s, me, slot).wait_recv()

    chunk = 256
    steps = width // chunk

    def chunked(body):
        def step(c, carry):
            body(pl.ds(pl.multiple_of(c * chunk, chunk), chunk), c)
            return carry
        lax.fori_loop(0, steps, step, 0)

    def run(b):
        values = tok.at[b]

        def scale(c):
            s = share[c * 2 // steps, b]
            return jnp.concatenate([s, s], 1)

        if forward:
            def ahead(cols, c):
                gt = dot(values[...], w[0, cols], (1,), (1,))
                u = dot(values[...], w[1, cols], (1,), (1,))
                gate[b, :, cols] = gt.astype(BF)
                up[b, :, cols] = u.astype(BF)
                act[b, :, cols] = (gt * jax.nn.sigmoid(gt) * u * scale(c)).astype(BF)

            chunked(ahead)

            def down(cols, c):
                part[b, :, cols] = dot(act[b], w[2, :, cols], (1,), (0,)).astype(BF)

            chunked(down)
            if not backward:
                for i, (a, o) in enumerate(zip((tok, act, gate, up), outs)):
                    pltpu.make_async_copy(a.at[b], o.at[b], save_sem.at[i, b]).start()
            else:
                save = pltpu.make_async_copy(part.at[b], part_out.at[b], save_sem.at[0, b])
                save.start()
                save.wait()
        if backward:
            source = second.at[b] if forward else values

            def back(cols, c):
                da = dot(source[...], w[2, cols], (1,), (1,)) * scale(c)
                gt, u = gate[b, :, cols].astype(F32), up[b, :, cols].astype(F32)
                sig = jax.nn.sigmoid(gt)
                gate[b, :, cols] = (da * u * sig * (1.0 + gt * (1.0 - sig))).astype(BF)
                up[b, :, cols] = (da * gt * sig).astype(BF)

            chunked(back)

            def mix(cols, c):
                total = dot(gate[b], w[0, :, cols], (1,), (0,)) + dot(up[b], w[1, :, cols], (1,), (0,))
                part[b, :, cols] = total.astype(BF)

            chunked(mix)

    def turn(i, carry):
        d = (i + 1) // 2
        b = me + jnp.where(i % 2 == 1, d, -d)

        @pl.when((b >= 0) & (b < n))
        def _():
            @pl.when(i > 0)
            def _():
                move(b, me, 0).wait_recv()

            @pl.when((me < n - 1) & (b <= me))
            def _():
                move(b, me + 1, 0).start()

            @pl.when((me > 0) & (b >= me))
            def _():
                move(b, me - 1, 1).start()

            @pl.when(i == 0)
            def _():
                for k in range(3):
                    pltpu.make_async_copy(w.at[k], w.at[k], w_sem.at[k]).wait()
                for load in loads:
                    load.wait()

            run(b)

            @pl.when((b > me) & (me == 0))
            def _():
                for s in range(SUB):
                    right(b, s).start()

            @pl.when((b < me) & (me == n - 1))
            def _():
                for s in range(SUB):
                    left(b, s).start()

        return carry

    lax.fori_loop(0, 2 * n - 1, turn, 0)

    piece = 2 * small
    slices = width // piece
    total = 3 * slices

    def save_slice(k, slot, out=0):
        unit = 2 * (k % (slices // 2))
        return [
            pltpu.make_async_copy(
                stage.at[slot, pl.ds(v * small, small)], gw_outs[out].at[unit + v, k // slices], save_sem.at[1 + v, slot]
            )
            for v in range(2)
        ]

    def weight_slice(k):
        slot = k % 2
        at = pl.ds(pl.multiple_of(k % slices * piece, HEAD), piece)

        @pl.when(k >= 2)
        def _():
            for copy in save_slice(k - 2, slot):
                copy.wait()

        tokens, grads = (tok, second) if forward else (second, tok)
        for i, (a, v) in enumerate(((gate, tokens), (up, tokens), (act, grads))):
            @pl.when(k // slices == i)
            def _():
                lhs = jnp.concatenate([a[b, :, at] for b in range(n)], 0)
                for c in range(2):
                    cols = pl.ds(c * (width // 2), width // 2)
                    rhs = jnp.concatenate([v[b, :, cols] for b in range(n)], 0)
                    stage[slot, :, cols] = dot(lhs, rhs, (0,), (0,)).astype(BF)

        for out in range(2):
            @pl.when(k % slices // (slices // 2) == out)
            def _():
                for copy in save_slice(k, slot, out):
                    copy.start()

    def add_rows(b, s, slot):
        at = pl.ds(pl.multiple_of(s * sub, sub), sub)
        part[b, at] = (part[b, at].astype(F32) + got[slot, at].astype(F32)).astype(BF)

    count = (n - 1) * SUB

    def relay(t, carry):
        q, s = 1 + t // SUB, t % SUB

        @pl.when((me > 0) & (q > me))
        def _():
            arrived(q, s, q)
            add_rows(q, s, q)
            right(q, s).start()

        @pl.when((me < n - 1) & (n - 1 - q < me))
        def _():
            b = n - 1 - q
            arrived(b, s, b)
            add_rows(b, s, b)
            left(b, s).start()

        if backward:
            def some(k, carry):
                weight_slice(k)
                return carry
            lax.fori_loop(t * total // count, (t + 1) * total // count, some, 0)
        return carry

    lax.fori_loop(0, count, relay, 0)
    y[...] = part[me].astype(F32)

    @pl.when(me > 0)
    def _():
        for s in range(SUB):
            arrived(me, s, me)
        y[...] += got[me].astype(F32)

    @pl.when(me < n - 1)
    def _():
        for s in range(SUB):
            arrived(me, s, n)
        y[...] += got[n].astype(F32)

    if backward:
        for k in (total - 2, total - 1):
            for copy in save_slice(k, k % 2):
                copy.wait()
    for b in range(n):
        if not backward:
            for i, (a, o) in enumerate(zip((tok, act, gate, up), outs)):
                pltpu.make_async_copy(a.at[b], o.at[b], save_sem.at[i, b]).wait()

        @pl.when((me < n - 1) & (b <= me))
        def _():
            move(b, me + 1, 0).wait_send()

        @pl.when((me > 0) & (b >= me))
        def _():
            move(b, me - 1, 1).wait_send()

        @pl.when(b > me)
        def _():
            for s in range(SUB):
                right(b, s).wait_send()

        @pl.when(b < me)
        def _():
            for s in range(SUB):
                left(b, s).wait_send()


def experts(n, forward, backward, x, share, small, pieces, *more):
    rows, width = x.shape
    hidden = small * 8
    shape = lambda *dims: jax.ShapeDtypeStruct(dims, BF)
    whole, wide = shape(n, rows, width), shape(n, rows, hidden)
    out = [jax.ShapeDtypeStruct((rows, width), F32)]
    out += [] if backward else [whole, wide, wide, wide]
    out += [whole] if forward and backward else []
    out += [shape(4, 3, small, width)] * 2 if backward else []
    room = lambda *dims: pltpu.VMEM(dims, BF)
    scratch = [room(n, rows, width), room(n, rows, width), room(n + 1, rows, width), room(3, hidden, width)]
    scratch += [room(n, rows, hidden)] * 3
    scratch += [room(n, rows, width), room(2, 2 * small, width)] if backward else []
    dma = pltpu.SemaphoreType.DMA
    scratch += [dma((2, n)), dma((n,)), dma((n, SUB)), dma((n + 1, SUB)), dma((3,)), dma((4,)), dma((4, n))]
    vmem, far = pl.BlockSpec(memory_space=pltpu.VMEM), pl.BlockSpec(memory_space=pl.ANY)
    return pl.pallas_call(
        functools.partial(expert_kernel, n, forward, backward),
        out_shape=out,
        in_specs=[vmem, vmem] + [far] * (8 + len(more)),
        out_specs=[vmem] + [far] * (len(out) - 1),
        scratch_shapes=scratch,
        compiler_params=pltpu.CompilerParams(
            collective_id=forward + 2 * backward, has_side_effects=True, vmem_limit_bytes=VMEM_LIMIT
        ),
        cost_estimate=pl.CostEstimate(flops=4 * 10**11, bytes_accessed=10**8, transcendentals=0),
    )(x, share, *pieces, *more)


def turn_head(values, cosine, sine):
    return values * cosine + pltpu.roll(values, HEAD // 2, 1) * sine


def head_group(i):
    own = i // 3
    return jnp.where(lax.axis_index(T) < 2, own, 1 - own)


def lanes(start, size=HEAD):
    return pl.ds(pl.multiple_of(start, HEAD), size)


def loop(count, body):
    def step(i, carry):
        body(i)
        return carry
    lax.fori_loop(0, count, step, 0)


def choose(mine, other, sem, *refs):
    first = lax.axis_index(S) == 0
    for i, (ref, low_first) in enumerate(refs):
        a, b = (mine, other) if low_first else (other, mine)

        @pl.when(first)
        def _():
            pltpu.make_async_copy(a, ref, sem.at[i]).start()

        @pl.when(jnp.logical_not(first))
        def _():
            pltpu.make_async_copy(b, ref, sem.at[i]).start()

    return [pltpu.make_async_copy(mine, ref, sem.at[i]) for i, (ref, _) in enumerate(refs)]


def attend_kernel(
    x, normed, kv, bias, cosine, sine, gain, mine, other, hidden, mixer, queries, flat, logs, wq, wo, sem
):
    pair = 2 * HEAD
    waits = choose(mine, other, sem, (wq, True), (wo, False))
    waits[0].wait()

    def heads(i):
        both = dot(normed[...], wq[lanes(i * pair, pair)], (1,), (1,))
        g = head_group(i)
        keys, values = kv[:, lanes(g * HEAD)], kv[:, lanes((GROUPS + g) * HEAD)]
        for j in range(2):
            at = lanes(i * pair + j * HEAD)
            q = turn_head(both[:, j * HEAD : (j + 1) * HEAD], cosine[...], sine[...]).astype(BF)
            queries[:, at] = q
            scores = dot(q, keys, (1,), (1,)) * HEAD ** (-0.5) + bias[...]
            peak = jnp.max(scores, 1, keepdims=True)
            raised = jnp.exp(scores - peak)
            total = jnp.sum(raised, 1, keepdims=True)
            probs = (raised * (1.0 / total)).astype(BF)
            flat[:, at] = dot(probs, values, (1,), (0,)).astype(BF)
            logs[:, at] = jnp.broadcast_to(peak + jnp.log(total), q.shape)

    loop(HEADS // 2, heads)

    waits[1].wait()

    def out(i):
        cols = lanes(i * pair, pair)
        hidden[:, cols] = x[:, cols].astype(F32) + dot(flat[...], wo[:, cols], (1,), (0,))

    loop(x.shape[1] // pair, out)
    h = hidden[...]
    mixer[...] = (h * inverse_rms(h) * gain[...]).astype(BF)


def attend_back_kernel(
    grad, grad_mixer, hidden, gain, queries, kv, logs, bias, flat, cosine, sine, mine, other,
    grad_hidden, gql, gkv, gwo, grad_gain, gao, ga, acc, wo, sem,
):
    pair = 2 * HEAD
    waits = choose(mine, other, sem, (wo, False))
    scale = HEAD ** (-0.5)
    h = hidden[...]
    r = inverse_rms(h)
    n = h * r
    grad_gain[...] = jnp.sum(grad_mixer[...] * n, 0, keepdims=True)
    m = grad_mixer[...] * gain[...]
    total = grad[...] + r * (m - n * jnp.mean(m * n, -1, keepdims=True))
    grad_hidden[...] = total
    gao[...] = total.astype(BF)
    acc[...] = jnp.zeros_like(acc)
    waits[0].wait()

    def heads(i):
        rows = lanes(i * pair, pair)
        ga[...] = dot(gao[...], wo[rows], (1,), (1,)).astype(BF)
        gwo[rows] = dot(flat[:, rows], gao[...], (0,), (0,)).astype(BF)
        g = head_group(i)
        key_at, value_at = lanes(g * HEAD), lanes((GROUPS + g) * HEAD)
        keys, values = kv[:, key_at], kv[:, value_at]
        for j in range(2):
            at = lanes(i * pair + j * HEAD)
            q, go = queries[:, at], ga[:, j * HEAD : (j + 1) * HEAD]
            scores = dot(q, keys, (1,), (1,)) * scale + bias[...]
            soft = jnp.exp(scores - logs[:, at][:, :1])
            grad_probs = dot(go, values, (1,), (1,))
            inner = jnp.sum(soft * grad_probs, 1, keepdims=True)
            gs = (soft * (grad_probs - inner)).astype(BF)
            gq = dot(gs, keys, (1,), (0,)) * scale
            gql[:, at] = turn_head(gq, cosine[...], -sine[...]).astype(BF)
            acc[:, key_at] += dot(gs, q, (0,), (0,)) * scale
            acc[:, value_at] += dot(soft.astype(BF), go, (0,), (0,))

    loop(HEADS // 2, heads)
    gkv[...] = acc[...].astype(BF)


def local_call(body, flops, out, scratch, *operands):
    return pl.pallas_call(
        body,
        out_shape=[jax.ShapeDtypeStruct(*o) for o in out],
        in_specs=[pl.BlockSpec(memory_space=pltpu.VMEM)] * (len(operands) - 2) + [pl.BlockSpec(memory_space=pl.ANY)] * 2,
        scratch_shapes=[pltpu.VMEM(*s) for s in scratch] + [pltpu.SemaphoreType.DMA((2,))],
        compiler_params=pltpu.CompilerParams(vmem_limit_bytes=VMEM_LIMIT),
        cost_estimate=pl.CostEstimate(flops=flops, bytes_accessed=2 * 10**7, transcendentals=0),
    )(*operands)


def keys_and_values(x, p, c, *before):
    rows = x.shape[0]
    xf = x.astype(F32)
    normed = low(xf * inverse_rms(xf) * p["ga"])
    kv = dot(normed, p["kv"], (1,), (0,)).reshape(rows, 2 * GROUPS, HEAD)
    cosine, sine = c["rope"]
    keys = rotate(kv[:, :GROUPS], cosine[:, None], sine[:, None])
    kv = low(jnp.concatenate([keys, kv[:, GROUPS:]], 1)).reshape(rows, -1)
    return normed, jnp.concatenate(pieces_of(after(kv, *before)))


def attention_forward(x, normed, kv, p, c):
    rows, width = x.shape
    cosine, sine = c["rope"]
    wide = (rows, HEADS * HEAD)
    hidden, mixer, queries, flat, logs = local_call(
        attend_kernel, 10**11, [((rows, width), F32), ((rows, width), BF), (wide, BF), (wide, BF), (wide, F32)],
        [(p["mine"].shape, BF)] * 2,
        x, normed, kv, c["bias"], cosine, sine, p["gm"].reshape(1, -1), p["mine"], p["other"],
    )
    kept = dict(x=x, normed=normed, kv=kv, queries=queries, logs=logs, flat=flat, hidden=hidden)
    return hidden, mixer, kept


def along(values):
    return lax.all_gather(low(values), D, axis=0, tiled=True)


def scatter_along(values):
    return lax.psum_scatter(low(values.reshape(-1, values.shape[-1])), D, scatter_dimension=0, tiled=True)


def weights_of(p):
    f = jnp.stack([v[-3 * p["unit"] :].reshape(3, p["unit"], -1) for v in p["pieces"]])
    return tuple(f[:, i].reshape(-1, f.shape[-1]) for i in range(3))


def share_of(p, hidden):
    return jnp.repeat(p["share"], hidden // 2, axis=1)


def mix_forward(mixer, p, n):
    if n <= SMALL:
        y, tokens, act, gate, up = experts(n, True, False, mixer, p["wide"], p["unit"], p["pieces"])
        return y, dict(tokens=tokens, act=act, gate=gate, up=up)
    wg, wu, wd = weights_of(p)
    tokens = along(mixer)
    gate, up = dot(tokens, wg, (1,), (1,)), dot(tokens, wu, (1,), (1,))
    act = low((jax.nn.silu(gate) * up * share_of(p, wd.shape[0])))
    y = scatter_along(dot(act, wd, (1,), (0,))).astype(F32)
    return y, dict(tokens=tokens, act=act, gate=low(gate), up=low(up))


def mix_backward(grad, k, p, n):
    if n <= SMALL:
        saved = (k["gate"], k["up"], k["act"], k["tokens"])
        return experts(n, False, True, grad, p["wide"], p["unit"], p["pieces"], *saved)
    wg, wu, wd = weights_of(p)
    grads = along(grad)
    da = dot(grads, wd, (1,), (1,)) * share_of(p, wd.shape[0])
    gate, up = k["gate"].astype(F32), k["up"].astype(F32)
    sig = jax.nn.sigmoid(gate)
    dg, du = low((da * up * sig * (1.0 + gate * (1.0 - sig)))), low((da * gate * sig))
    gm = scatter_along(dot(dg, wg, (1,), (0,)) + dot(du, wu, (1,), (0,))).astype(F32)
    flat = lambda v: v.reshape(-1, v.shape[-1])
    pairs = ((dg, k["tokens"]), (du, k["tokens"]), (k["act"], grads))
    gw = [low(dot(flat(u), flat(v), (0,), (0,))) for u, v in pairs]
    gw = jnp.stack([g.reshape(8, -1, g.shape[-1]) for g in gw], 1)
    return gm, gw[:4], gw[4:]


def mix_both(mixer, grad, p, n, grads):
    if n <= SMALL:
        grads = grads.reshape(n, *grad.shape)
        gm, part, keep, give = experts(n, True, True, mixer, p["wide"], p["unit"], p["pieces"], grads)
        return part, gm, keep, give
    y, k = mix_forward(mixer, p, n)
    return (y,) + mix_backward(grad, k, p, n)


def attention_backward(grad, grad_mixer, k, p, c, first):
    rows, width = grad.shape
    cosine, sine = c["rope"]
    wide, length = (rows, HEADS * HEAD), c["bias"].shape[1]
    grad_hidden, gql, gkv, gw_out, g_gm = local_call(
        attend_back_kernel, 10**11,
        [((rows, width), F32), (wide, BF), ((length, 2 * GROUPS * HEAD), BF), ((HEADS * HEAD, width), BF), ((1, width), F32)],
        [((rows, width), BF), ((rows, 2 * HEAD), BF), ((length, 2 * GROUPS * HEAD), F32), (p["mine"].shape, BF)],
        grad, grad_mixer, k["hidden"], p["gm"].reshape(1, -1), k["queries"], k["kv"], k["logs"], c["bias"],
        k["flat"], cosine, sine, p["mine"], p["other"],
    )
    gkv = gkv.reshape(4, rows, -1)
    gkv = gkv[0].astype(F32) + sum(hop(gkv[r], r).astype(F32) for r in (1, 2, 3))
    gkv = gkv.reshape(rows, 2 * GROUPS, HEAD)
    cosine, sine = cosine[:, None], sine[:, None]
    gkv = jnp.concatenate([rotate(gkv[:, :GROUPS], cosine, -sine), gkv[:, GROUPS:]], 1)
    gkv = low(gkv).reshape(rows, -1)
    wq = jnp.where(first, p["mine"], p["other"])
    grad_normed = dot(gql, wq, (1,), (0,)) + dot(gkv, p["kv"], (1,), (1,))
    gw_q = low(dot(gql, k["normed"], (0,), (0,)))
    gw_kv = dot(gkv, k["normed"], (0,), (0,))
    more, g_ga = norm_back(grad_normed, k["x"].astype(F32), p["ga"])
    gw_kv = gw_kv.reshape(2, -1, width)
    at = lax.axis_index(T)
    pad = jnp.zeros((63, width), F32)

    def rows_of(main, i, gain):
        less = low(jnp.concatenate([gw_kv[i], gain[None], pad])).reshape(4, -1, width)
        less = jnp.stack([lax.dynamic_index_in_dim(less, at ^ r, 0, False) for r in range(4)])
        return jnp.concatenate([main.reshape(4, -1, width), less], 1)

    q, o = rows_of(gw_q, 0, g_ga), rows_of(gw_out, 1, g_gm[0])
    parts = over_sections(jnp.where(first, q, o), jnp.where(first, o, q))
    return grad_hidden + more, parts


def on_device(
    inputs, cotangent, segments, routes, route_gates, attn_gain, w_query, key_weight,
    value_weight, w_out, mixer_gain, w_gate, w_up, w_down,
):
    section = lax.axis_index(S)
    first = section == 0
    at = lax.axis_index(T)
    rows, width = inputs.shape[1:]
    length = segments.shape[2]
    here = w_gate.shape[1]
    hidden = w_gate.shape[3]
    experts = lax.axis_size(D) * here
    mine = lambda a: lax.dynamic_index_in_dim(a, section, 0, False)
    theirs = lambda a: lax.dynamic_index_in_dim(a, 1 - section, 0, False)
    x0 = mine(inputs)
    grad1 = mine(cotangent)
    segment = mine(segments)[0]

    def halves(own):
        keep, got = mine(own), partner(theirs(own))
        return jnp.where(first, keep, got), jnp.where(first, got, keep)

    named = routes[0][..., None] == jnp.arange(experts, dtype=jnp.int32)
    shares = jnp.sum(jnp.where(named, route_gates[0][..., None], 0.0), 2)
    shares = jnp.stack(halves(shares), 1)

    shares = line_gather(shares)

    def factors(own, l):
        share = own[:, l]
        share = lax.dynamic_slice_in_dim(share, lax.axis_index(D) * here, here, 1)
        share = jnp.stack([jnp.where(first, share[:, i], share[:, 1 - i]) for i in range(2)], 1)
        return jnp.broadcast_to(share.T.reshape(here, -1, rows, 1), (here, share.shape[0] // rows, rows, HEAD)), share

    queries_at = at * rows + jnp.arange(rows)
    keys_at = jnp.concatenate([(at ^ r) * rows + jnp.arange(rows) for r in range(4)])
    key_segment = jnp.concatenate([lax.dynamic_slice_in_dim(segment, (at ^ r) * rows, rows, 0) for r in range(4)])
    allowed = (keys_at[None] <= queries_at[:, None]) & (key_segment[:rows, None] == key_segment[None])
    c = dict(rope=rope_tables(queries_at.astype(F32)), bias=jnp.where(allowed, 0.0, -1e30))

    attn = halves(jnp.stack([w_query[0].T, w_out[0]]))
    g, u = (w[0].transpose(0, 2, 1) for w in (w_gate, w_up))
    ffn = halves(jnp.stack([g, u, w_down[0]], 1))
    kv = both(first, jnp.concatenate([key_weight[0], value_weight[0]], 1))
    ga = both(first, attn_gain)
    gm = both(first, mixer_gain)
    n = lax.axis_size(D)
    small = [dict(kv=kv[l], ga=ga[l], gm=gm[l], unit=hidden) for l in range(2)]
    for l, one in enumerate(small):
        one["wide"], one["share"] = factors(shares, l)
    grads = along(low(grad1)) if n <= SMALL else low(grad1)
    ffn = [v.reshape(-1, width) for v in ffn]
    high = w_out.shape[1]

    ahead = keys_and_values(x0, small[0], c)
    got = pieces_of(attn[0])
    late = after(ffn[0], got, ahead, grads)
    mine = jnp.concatenate(got)
    small[0].update(mine=mine, other=partner(mine))
    hidden0, mixer, k0 = attention_forward(x0, *ahead, small[0], c)
    got = pieces_of(late)
    crossed = after(got, mixer)
    small[0].update(pieces=got + [partner(v) for v in crossed])
    more = pieces_of(after(jnp.concatenate([attn[1], ffn[1]]), got))
    y, kept = mix_forward(mixer, small[0], n)
    y0 = low((hidden0 + y))
    other = [partner(v) for v in after(more, y)]
    small[1].update(
        mine=jnp.concatenate([v[:high] for v in more]), other=jnp.concatenate([v[:high] for v in other]),
        pieces=more + other,
    )
    hidden1, mixer, k1 = attention_forward(y0, *keys_and_values(y0, small[1], c, other), small[1], c)
    y, gm, keep, give = mix_both(mixer, low(grad1), small[1], n, grads)
    parts = over_sections(keep, give)
    gx1, more = attention_backward(grad1, gm, k1, small[1], c, first)
    gb = low(gx1)
    rows_f = 3 * hidden
    both_parts = [jnp.concatenate([a.reshape(rows_f, width), b]) for a, b in zip(parts, more)]
    gb, both_parts = lax.optimization_barrier((gb, both_parts))
    got = summed(both_parts)
    gm, keep, give = mix_backward(gb, kept, small[0], n)
    gm, got, y = lax.optimization_barrier((gm, got, y))
    y1 = low(hidden1 + (scatter_along(y).astype(F32) if n <= SMALL else y))
    f1, s1 = got[:rows_f].reshape(3, hidden, width), lax.psum(got[rows_f:], D)
    parts = over_sections(keep, give)
    gx0, more = attention_backward(gb.astype(F32), gm, k0, small[0], c, first)
    s0 = summed(more)
    f0 = summed(after(parts, s0))
    s0 = lax.psum(after(s0, s1, y1), D)

    outs = jnp.stack(swap(first, y0, y1))
    input_grads = jnp.stack(swap(first, low(gx0), low(gx1))).astype(F32)
    f = jnp.stack(swap(first, f0, f1)).astype(F32)
    zero, one = swap(first, s0, s1)
    q, o = zero[:high].astype(F32), one[:high].astype(F32)
    less = jnp.stack(pieces_of(jnp.stack([zero[high:], one[high:]])))
    less = jnp.concatenate([lax.dynamic_index_in_dim(less, at ^ i, 0, False) for i in range(4)], 1).astype(F32)
    ka, vm = less[0], less[1]
    few = GROUPS * HEAD
    return (
        outs[None], input_grads[None], ka[few : few + 1], q.T[None], ka[:few].T[None],
        vm[:few].T[None], o[None], vm[few : few + 1], f[:, 0].transpose(0, 2, 1)[None],
        f[:, 1].transpose(0, 2, 1)[None], f[:, 2][None],
    )


def solution(mesh):
    rows, layer, cols = P(None, (D, T), None), P(S, None, (D, T), None), P(S, D, None, T)
    in_specs = (
        rows, rows, P(None, D, None), layer, layer, P(S, None), P(S, None, T), P(S, None, None),
        P(S, None, None), P(S, T, None), P(S, None), cols, cols, P(S, D, T, None),
    )
    out_specs = (
        layer, layer, P(S, None), P(S, None, T), P(S, None, None), P(S, None, None), P(S, T, None),
        P(S, None), cols, cols, P(S, D, T, None),
    )
    return jax.shard_map(on_device, mesh=mesh, in_specs=in_specs, out_specs=out_specs, check_vma=False)
```

```python
import functools
import jax
import jax.numpy as jnp
from jax import lax
from jax.experimental import pallas as pl
from jax.experimental.pallas import tpu as pltpu
from jax.sharding import PartitionSpec as P

S, D, T = "section", "dp", "tensor"
HEADS = 12
GROUPS = 2
HEAD = 128
EPSILON = 1e-06
BF = jnp.bfloat16
F32 = jnp.float32


def dot(a, b, ca, cb):
    return lax.dot_general(a, b, ((ca, cb), ((), ())), preferred_element_type=F32)


def low(values):
    return lax.reduce_precision(values.astype(F32), 8, 7).astype(BF)


def partner(values):
    return lax.ppermute(values, S, [(0, 1), (1, 0)])


def both(first, own):
    other = partner(own)
    return jnp.where(first, own, other), jnp.where(first, other, own)


def swap(first, zero, one):
    keep = jnp.where(first, zero, one)
    got = partner(jnp.where(first, one, zero))
    return jnp.where(first, keep, got), jnp.where(first, got, keep)


def hop(values, bit):
    return lax.ppermute(values, T, [(i, i ^ bit) for i in range(lax.axis_size(T))])


def after(values, *others):
    return lax.optimization_barrier((values, others))[0]


def line_gather(own):
    n, me = lax.axis_size(D), lax.axis_index(D)
    if n != SMALL:
        return lax.all_gather(own, D, axis=0, tiled=True)
    got = [own] + [lax.ppermute(own, D, [(i, i ^ r) for i in range(n)]) for r in range(1, n)]
    got = jnp.stack(got)
    return jnp.concatenate([lax.dynamic_index_in_dim(got, me ^ b, 0, False) for b in range(n)])


def pieces_of(own):
    return [own] + [hop(own, r) for r in (1, 2, 3)]


def add(*values):
    return low(sum(v.astype(F32) for v in values))


def summed(parts):
    return add(parts[0], *(hop(parts[r], r) for r in (1, 2, 3)))


def over_sections(keep, give):
    got = partner(give)
    return [add(keep[r], got[r]) for r in range(4)]


def rope_tables(places):
    half = HEAD // 2
    rates = 10000.0 ** (-jnp.arange(half, dtype=F32) * 2.0 / HEAD)
    angles = places[:, None] * rates[None, :]
    cosine, sine = jnp.cos(angles), jnp.sin(angles)
    return jnp.concatenate([cosine, cosine], 1), jnp.concatenate([-sine, sine], 1)


def rotate(values, cosine, sine):
    half = HEAD // 2
    turned = jnp.concatenate([values[..., half:], values[..., :half]], -1)
    return values * cosine + turned * sine


def inverse_rms(values):
    return lax.rsqrt(jnp.mean(values * values, -1, keepdims=True) + EPSILON)


def norm_back(grad, values, gain):
    r = inverse_rms(values)
    n = values * r
    m = grad * gain
    return r * (m - n * jnp.mean(m * n, -1, keepdims=True)), jnp.sum(grad * n, 0)


MESH = pl.DeviceIdType.MESH
SMALL = 4
SUB = 4
VMEM_LIMIT = 48 * 1024 * 1024


def expert_kernel(n, forward, backward, *refs):
    refs = list(refs)
    take = lambda count: [refs.pop(0) for _ in range(count)]
    x, share = take(2)
    pieces = take(8)
    grads_in = take(1)[0] if forward and backward else None
    saved = take(4) if not forward else None
    y = take(1)[0]
    outs = take(4) if not backward else None
    part_out = take(1)[0] if forward and backward else None
    gw_outs = take(2) if backward else None
    tok, part, got, w, gate, up, act = take(7)
    second = take(1)[0] if backward else None
    stage = take(1)[0] if backward else None
    tok_send, tok_recv, part_send, part_recv, w_sem, io_sem, save_sem = refs
    rows, width = x.shape
    sub = rows // SUB
    me = lax.axis_index(D)

    small = w.shape[1] // 8
    for i in range(3):
        for k, one in enumerate(pieces):
            rows_at = pl.ds(one.shape[0] - (3 - i) * small, small)
            pltpu.make_async_copy(one.at[rows_at], w.at[i, pl.ds(k * small, small)], w_sem.at[i]).start()
    loads = []
    if saved is not None:
        loads = [pltpu.make_async_copy(a, o, io_sem.at[i]) for i, (a, o) in enumerate(zip(saved, (gate, up, act, second)))]
    elif backward:
        loads = [pltpu.make_async_copy(grads_in, second, io_sem.at[0])]
    for load in loads:
        load.start()
    barrier = pltpu.get_barrier_semaphore()
    for step in (-1, 1):
        @pl.when((me + step >= 0) & (me + step < n))
        def _():
            pl.semaphore_signal(barrier, inc=1, device_id={D: me + step}, device_id_type=MESH)
    tok[me] = x[...]
    pl.semaphore_wait(barrier, jnp.where((me == 0) | (me == n - 1), 1, 2))

    def move(b, to, side):
        return pltpu.make_async_remote_copy(
            src_ref=tok.at[b], dst_ref=tok.at[b], send_sem=tok_send.at[side, b], recv_sem=tok_recv.at[b],
            device_id={D: to}, device_id_type=MESH,
        )

    def pass_sum(b, s, to, slot):
        at = pl.ds(pl.multiple_of(s * sub, sub), sub)
        return pltpu.make_async_remote_copy(
            src_ref=part.at[b, at], dst_ref=got.at[slot, at], send_sem=part_send.at[b, s],
            recv_sem=part_recv.at[slot, s], device_id={D: to}, device_id_type=MESH,
        )

    def right(b, s):
        return pass_sum(b, s, me + 1, b)

    def left(b, s):
        return pass_sum(b, s, me - 1, jnp.where(b == me - 1, n, b))

    def arrived(b, s, slot):
        pass_sum(b, s, me, slot).wait_recv()

    chunk = 256
    steps = width // chunk

    def chunked(body):
        def step(c, carry):
            body(pl.ds(pl.multiple_of(c * chunk, chunk), chunk), c)
            return carry
        lax.fori_loop(0, steps, step, 0)

    def run(b):
        values = tok.at[b]

        def scale(c):
            s = share[c * 2 // steps, b]
            return jnp.concatenate([s, s], 1)

        if forward:
            def ahead(cols, c):
                gt = dot(values[...], w[0, cols], (1,), (1,))
                u = dot(values[...], w[1, cols], (1,), (1,))
                gate[b, :, cols] = gt.astype(BF)
                up[b, :, cols] = u.astype(BF)
                act[b, :, cols] = (gt * jax.nn.sigmoid(gt) * u * scale(c)).astype(BF)

            chunked(ahead)

            def down(cols, c):
                part[b, :, cols] = dot(act[b], w[2, :, cols], (1,), (0,)).astype(BF)

            chunked(down)
            if not backward:
                for i, (a, o) in enumerate(zip((tok, act, gate, up), outs)):
                    pltpu.make_async_copy(a.at[b], o.at[b], save_sem.at[i, b]).start()
            else:
                save = pltpu.make_async_copy(part.at[b], part_out.at[b], save_sem.at[0, b])
                save.start()
                save.wait()
        if backward:
            source = second.at[b] if forward else values

            def back(cols, c):
                da = dot(source[...], w[2, cols], (1,), (1,)) * scale(c)
                gt, u = gate[b, :, cols].astype(F32), up[b, :, cols].astype(F32)
                sig = jax.nn.sigmoid(gt)
                gate[b, :, cols] = (da * u * sig * (1.0 + gt * (1.0 - sig))).astype(BF)
                up[b, :, cols] = (da * gt * sig).astype(BF)

            chunked(back)

            def mix(cols, c):
                total = dot(gate[b], w[0, :, cols], (1,), (0,)) + dot(up[b], w[1, :, cols], (1,), (0,))
                part[b, :, cols] = total.astype(BF)

            chunked(mix)

    def turn(i, carry):
        d = (i + 1) // 2
        b = me + jnp.where(i % 2 == 1, d, -d)

        @pl.when((b >= 0) & (b < n))
        def _():
            @pl.when(i > 0)
            def _():
                move(b, me, 0).wait_recv()

            @pl.when((me < n - 1) & (b <= me))
            def _():
                move(b, me + 1, 0).start()

            @pl.when((me > 0) & (b >= me))
            def _():
                move(b, me - 1, 1).start()

            @pl.when(i == 0)
            def _():
                for k in range(3):
                    pltpu.make_async_copy(w.at[k], w.at[k], w_sem.at[k]).wait()
                for load in loads:
                    load.wait()

            run(b)

            @pl.when((b > me) & (me == 0))
            def _():
                for s in range(SUB):
                    right(b, s).start()

            @pl.when((b < me) & (me == n - 1))
            def _():
                for s in range(SUB):
                    left(b, s).start()

        return carry

    lax.fori_loop(0, 2 * n - 1, turn, 0)

    piece = 2 * small
    slices = width // piece
    total = 3 * slices

    def save_slice(k, slot, out=0):
        unit = 2 * (k % (slices // 2))
        return [
            pltpu.make_async_copy(
                stage.at[slot, pl.ds(v * small, small)], gw_outs[out].at[unit + v, k // slices], save_sem.at[1 + v, slot]
            )
            for v in range(2)
        ]

    def weight_slice(k):
        slot = k % 2
        at = pl.ds(pl.multiple_of(k % slices * piece, HEAD), piece)

        @pl.when(k >= 2)
        def _():
            for copy in save_slice(k - 2, slot):
                copy.wait()

        tokens, grads = (tok, second) if forward else (second, tok)
        for i, (a, v) in enumerate(((gate, tokens), (up, tokens), (act, grads))):
            @pl.when(k // slices == i)
            def _():
                lhs = jnp.concatenate([a[b, :, at] for b in range(n)], 0)
                for c in range(2):
                    cols = pl.ds(c * (width // 2), width // 2)
                    rhs = jnp.concatenate([v[b, :, cols] for b in range(n)], 0)
                    stage[slot, :, cols] = dot(lhs, rhs, (0,), (0,)).astype(BF)

        for out in range(2):
            @pl.when(k % slices // (slices // 2) == out)
            def _():
                for copy in save_slice(k, slot, out):
                    copy.start()

    def add_rows(b, s, slot):
        at = pl.ds(pl.multiple_of(s * sub, sub), sub)
        part[b, at] = (part[b, at].astype(F32) + got[slot, at].astype(F32)).astype(BF)

    count = (n - 1) * SUB

    def relay(t, carry):
        q, s = 1 + t // SUB, t % SUB

        @pl.when((me > 0) & (q > me))
        def _():
            arrived(q, s, q)
            add_rows(q, s, q)
            right(q, s).start()

        @pl.when((me < n - 1) & (n - 1 - q < me))
        def _():
            b = n - 1 - q
            arrived(b, s, b)
            add_rows(b, s, b)
            left(b, s).start()

        if backward:
            def some(k, carry):
                weight_slice(k)
                return carry
            lax.fori_loop(t * total // count, (t + 1) * total // count, some, 0)
        return carry

    lax.fori_loop(0, count, relay, 0)
    y[...] = part[me].astype(F32)

    @pl.when(me > 0)
    def _():
        for s in range(SUB):
            arrived(me, s, me)
        y[...] += got[me].astype(F32)

    @pl.when(me < n - 1)
    def _():
        for s in range(SUB):
            arrived(me, s, n)
        y[...] += got[n].astype(F32)

    if backward:
        for k in (total - 2, total - 1):
            for copy in save_slice(k, k % 2):
                copy.wait()
    for b in range(n):
        if not backward:
            for i, (a, o) in enumerate(zip((tok, act, gate, up), outs)):
                pltpu.make_async_copy(a.at[b], o.at[b], save_sem.at[i, b]).wait()

        @pl.when((me < n - 1) & (b <= me))
        def _():
            move(b, me + 1, 0).wait_send()

        @pl.when((me > 0) & (b >= me))
        def _():
            move(b, me - 1, 1).wait_send()

        @pl.when(b > me)
        def _():
            for s in range(SUB):
                right(b, s).wait_send()

        @pl.when(b < me)
        def _():
            for s in range(SUB):
                left(b, s).wait_send()


def experts(n, forward, backward, x, share, small, pieces, *more):
    rows, width = x.shape
    hidden = small * 8
    shape = lambda *dims: jax.ShapeDtypeStruct(dims, BF)
    whole, wide = shape(n, rows, width), shape(n, rows, hidden)
    out = [jax.ShapeDtypeStruct((rows, width), F32)]
    out += [] if backward else [whole, wide, wide, wide]
    out += [whole] if forward and backward else []
    out += [shape(4, 3, small, width)] * 2 if backward else []
    room = lambda *dims: pltpu.VMEM(dims, BF)
    scratch = [room(n, rows, width), room(n, rows, width), room(n + 1, rows, width), room(3, hidden, width)]
    scratch += [room(n, rows, hidden)] * 3
    scratch += [room(n, rows, width), room(2, 2 * small, width)] if backward else []
    dma = pltpu.SemaphoreType.DMA
    scratch += [dma((2, n)), dma((n,)), dma((n, SUB)), dma((n + 1, SUB)), dma((3,)), dma((4,)), dma((4, n))]
    vmem, far = pl.BlockSpec(memory_space=pltpu.VMEM), pl.BlockSpec(memory_space=pl.ANY)
    return pl.pallas_call(
        functools.partial(expert_kernel, n, forward, backward),
        out_shape=out,
        in_specs=[vmem, vmem] + [far] * (8 + len(more)),
        out_specs=[vmem] + [far] * (len(out) - 1),
        scratch_shapes=scratch,
        compiler_params=pltpu.CompilerParams(
            collective_id=forward + 2 * backward, has_side_effects=True, vmem_limit_bytes=VMEM_LIMIT
        ),
        cost_estimate=pl.CostEstimate(flops=4 * 10**11, bytes_accessed=10**8, transcendentals=0),
    )(x, share, *pieces, *more)


def turn_head(values, cosine, sine):
    return values * cosine + pltpu.roll(values, HEAD // 2, 1) * sine


def head_group(i):
    own = i // 3
    return jnp.where(lax.axis_index(T) < 2, own, 1 - own)


def lanes(start, size=HEAD):
    return pl.ds(pl.multiple_of(start, HEAD), size)


def loop(count, body):
    def step(i, carry):
        body(i)
        return carry
    lax.fori_loop(0, count, step, 0)


def choose(mine, other, sem, *refs):
    first = lax.axis_index(S) == 0
    for i, (ref, low_first) in enumerate(refs):
        a, b = (mine, other) if low_first else (other, mine)

        @pl.when(first)
        def _():
            pltpu.make_async_copy(a, ref, sem.at[i]).start()

        @pl.when(jnp.logical_not(first))
        def _():
            pltpu.make_async_copy(b, ref, sem.at[i]).start()

    return [pltpu.make_async_copy(mine, ref, sem.at[i]) for i, (ref, _) in enumerate(refs)]


def attend_kernel(
    x, normed, kv, bias, cosine, sine, gain, mine, other, hidden, mixer, queries, flat, logs, wq, wo, sem
):
    pair = 2 * HEAD
    waits = choose(mine, other, sem, (wq, True), (wo, False))
    waits[0].wait()

    def heads(i):
        both = dot(normed[...], wq[lanes(i * pair, pair)], (1,), (1,))
        g = head_group(i)
        keys, values = kv[:, lanes(g * HEAD)], kv[:, lanes((GROUPS + g) * HEAD)]
        for j in range(2):
            at = lanes(i * pair + j * HEAD)
            q = turn_head(both[:, j * HEAD : (j + 1) * HEAD], cosine[...], sine[...]).astype(BF)
            queries[:, at] = q
            scores = dot(q, keys, (1,), (1,)) * HEAD ** (-0.5) + bias[...]
            peak = jnp.max(scores, 1, keepdims=True)
            raised = jnp.exp(scores - peak)
            total = jnp.sum(raised, 1, keepdims=True)
            probs = (raised * (1.0 / total)).astype(BF)
            flat[:, at] = dot(probs, values, (1,), (0,)).astype(BF)
            logs[:, at] = jnp.broadcast_to(peak + jnp.log(total), q.shape)

    loop(HEADS // 2, heads)

    waits[1].wait()

    def out(i):
        cols = lanes(i * pair, pair)
        hidden[:, cols] = x[:, cols].astype(F32) + dot(flat[...], wo[:, cols], (1,), (0,))

    loop(x.shape[1] // pair, out)
    h = hidden[...]
    mixer[...] = (h * inverse_rms(h) * gain[...]).astype(BF)


def attend_back_kernel(
    grad, grad_mixer, hidden, gain, queries, kv, logs, bias, flat, cosine, sine, mine, other,
    grad_hidden, gql, gkv, gwo, grad_gain, gao, ga, acc, wo, sem,
):
    pair = 2 * HEAD
    waits = choose(mine, other, sem, (wo, False))
    scale = HEAD ** (-0.5)
    h = hidden[...]
    r = inverse_rms(h)
    n = h * r
    grad_gain[...] = jnp.sum(grad_mixer[...] * n, 0, keepdims=True)
    m = grad_mixer[...] * gain[...]
    total = grad[...] + r * (m - n * jnp.mean(m * n, -1, keepdims=True))
    grad_hidden[...] = total
    gao[...] = total.astype(BF)
    acc[...] = jnp.zeros_like(acc)
    waits[0].wait()

    def heads(i):
        rows = lanes(i * pair, pair)
        ga[...] = dot(gao[...], wo[rows], (1,), (1,)).astype(BF)
        gwo[rows] = dot(flat[:, rows], gao[...], (0,), (0,)).astype(BF)
        g = head_group(i)
        key_at, value_at = lanes(g * HEAD), lanes((GROUPS + g) * HEAD)
        keys, values = kv[:, key_at], kv[:, value_at]
        for j in range(2):
            at = lanes(i * pair + j * HEAD)
            q, go = queries[:, at], ga[:, j * HEAD : (j + 1) * HEAD]
            scores = dot(q, keys, (1,), (1,)) * scale + bias[...]
            soft = jnp.exp(scores - logs[:, at][:, :1])
            grad_probs = dot(go, values, (1,), (1,))
            inner = jnp.sum(soft * grad_probs, 1, keepdims=True)
            gs = (soft * (grad_probs - inner)).astype(BF)
            gq = dot(gs, keys, (1,), (0,)) * scale
            gql[:, at] = turn_head(gq, cosine[...], -sine[...]).astype(BF)
            acc[:, key_at] += dot(gs, q, (0,), (0,)) * scale
            acc[:, value_at] += dot(soft.astype(BF), go, (0,), (0,))

    loop(HEADS // 2, heads)
    gkv[...] = acc[...].astype(BF)


def local_call(body, flops, out, scratch, *operands):
    return pl.pallas_call(
        body,
        out_shape=[jax.ShapeDtypeStruct(*o) for o in out],
        in_specs=[pl.BlockSpec(memory_space=pltpu.VMEM)] * (len(operands) - 2) + [pl.BlockSpec(memory_space=pl.ANY)] * 2,
        scratch_shapes=[pltpu.VMEM(*s) for s in scratch] + [pltpu.SemaphoreType.DMA((2,))],
        compiler_params=pltpu.CompilerParams(vmem_limit_bytes=VMEM_LIMIT),
        cost_estimate=pl.CostEstimate(flops=flops, bytes_accessed=2 * 10**7, transcendentals=0),
    )(*operands)


def keys_and_values(x, p, c, *before):
    rows = x.shape[0]
    xf = x.astype(F32)
    normed = low(xf * inverse_rms(xf) * p["ga"])
    kv = dot(normed, p["kv"], (1,), (0,)).reshape(rows, 2 * GROUPS, HEAD)
    cosine, sine = c["rope"]
    keys = rotate(kv[:, :GROUPS], cosine[:, None], sine[:, None])
    kv = low(jnp.concatenate([keys, kv[:, GROUPS:]], 1)).reshape(rows, -1)
    return normed, jnp.concatenate(pieces_of(after(kv, *before)))


def attention_forward(x, normed, kv, p, c):
    rows, width = x.shape
    cosine, sine = c["rope"]
    wide = (rows, HEADS * HEAD)
    hidden, mixer, queries, flat, logs = local_call(
        attend_kernel, 10**11, [((rows, width), F32), ((rows, width), BF), (wide, BF), (wide, BF), (wide, F32)],
        [(p["mine"].shape, BF)] * 2,
        x, normed, kv, c["bias"], cosine, sine, p["gm"].reshape(1, -1), p["mine"], p["other"],
    )
    kept = dict(x=x, normed=normed, kv=kv, queries=queries, logs=logs, flat=flat, hidden=hidden)
    return hidden, mixer, kept


def along(values):
    return lax.all_gather(low(values), D, axis=0, tiled=True)


def scatter_along(values):
    return lax.psum_scatter(low(values.reshape(-1, values.shape[-1])), D, scatter_dimension=0, tiled=True)


def weights_of(p):
    f = jnp.stack([v[-3 * p["unit"] :].reshape(3, p["unit"], -1) for v in p["pieces"]])
    return tuple(f[:, i].reshape(-1, f.shape[-1]) for i in range(3))


def share_of(p, hidden):
    return jnp.repeat(p["share"], hidden // 2, axis=1)


def mix_forward(mixer, p, n):
    if n <= SMALL:
        y, tokens, act, gate, up = experts(n, True, False, mixer, p["wide"], p["unit"], p["pieces"])
        return y, dict(tokens=tokens, act=act, gate=gate, up=up)
    wg, wu, wd = weights_of(p)
    tokens = along(mixer)
    gate, up = dot(tokens, wg, (1,), (1,)), dot(tokens, wu, (1,), (1,))
    act = low((jax.nn.silu(gate) * up * share_of(p, wd.shape[0])))
    y = scatter_along(dot(act, wd, (1,), (0,))).astype(F32)
    return y, dict(tokens=tokens, act=act, gate=low(gate), up=low(up))


def mix_backward(grad, k, p, n):
    if n <= SMALL:
        saved = (k["gate"], k["up"], k["act"], k["tokens"])
        return experts(n, False, True, grad, p["wide"], p["unit"], p["pieces"], *saved)
    wg, wu, wd = weights_of(p)
    grads = along(grad)
    da = dot(grads, wd, (1,), (1,)) * share_of(p, wd.shape[0])
    gate, up = k["gate"].astype(F32), k["up"].astype(F32)
    sig = jax.nn.sigmoid(gate)
    dg, du = low((da * up * sig * (1.0 + gate * (1.0 - sig)))), low((da * gate * sig))
    gm = scatter_along(dot(dg, wg, (1,), (0,)) + dot(du, wu, (1,), (0,))).astype(F32)
    flat = lambda v: v.reshape(-1, v.shape[-1])
    pairs = ((dg, k["tokens"]), (du, k["tokens"]), (k["act"], grads))
    gw = [low(dot(flat(u), flat(v), (0,), (0,))) for u, v in pairs]
    gw = jnp.stack([g.reshape(8, -1, g.shape[-1]) for g in gw], 1)
    return gm, gw[:4], gw[4:]


def mix_both(mixer, grad, p, n, grads):
    if n <= SMALL:
        grads = grads.reshape(n, *grad.shape)
        gm, part, keep, give = experts(n, True, True, mixer, p["wide"], p["unit"], p["pieces"], grads)
        return part, gm, keep, give
    y, k = mix_forward(mixer, p, n)
    return (y,) + mix_backward(grad, k, p, n)


def attention_backward(grad, grad_mixer, k, p, c, first):
    rows, width = grad.shape
    cosine, sine = c["rope"]
    wide, length = (rows, HEADS * HEAD), c["bias"].shape[1]
    grad_hidden, gql, gkv, gw_out, g_gm = local_call(
        attend_back_kernel, 10**11,
        [((rows, width), F32), (wide, BF), ((length, 2 * GROUPS * HEAD), BF), ((HEADS * HEAD, width), BF), ((1, width), F32)],
        [((rows, width), BF), ((rows, 2 * HEAD), BF), ((length, 2 * GROUPS * HEAD), F32), (p["mine"].shape, BF)],
        grad, grad_mixer, k["hidden"], p["gm"].reshape(1, -1), k["queries"], k["kv"], k["logs"], c["bias"],
        k["flat"], cosine, sine, p["mine"], p["other"],
    )
    gkv = gkv.reshape(4, rows, -1)
    gkv = gkv[0].astype(F32) + sum(hop(gkv[r], r).astype(F32) for r in (1, 2, 3))
    gkv = gkv.reshape(rows, 2 * GROUPS, HEAD)
    cosine, sine = cosine[:, None], sine[:, None]
    gkv = jnp.concatenate([rotate(gkv[:, :GROUPS], cosine, -sine), gkv[:, GROUPS:]], 1)
    gkv = low(gkv).reshape(rows, -1)
    wq = jnp.where(first, p["mine"], p["other"])
    grad_normed = dot(gql, wq, (1,), (0,)) + dot(gkv, p["kv"], (1,), (1,))
    gw_q = low(dot(gql, k["normed"], (0,), (0,)))
    gw_kv = dot(gkv, k["normed"], (0,), (0,))
    more, g_ga = norm_back(grad_normed, k["x"].astype(F32), p["ga"])
    gw_kv = gw_kv.reshape(2, -1, width)
    at = lax.axis_index(T)
    pad = jnp.zeros((63, width), F32)

    def rows_of(main, i, gain):
        less = low(jnp.concatenate([gw_kv[i], gain[None], pad])).reshape(4, -1, width)
        less = jnp.stack([lax.dynamic_index_in_dim(less, at ^ r, 0, False) for r in range(4)])
        return jnp.concatenate([main.reshape(4, -1, width), less], 1)

    q, o = rows_of(gw_q, 0, g_ga), rows_of(gw_out, 1, g_gm[0])
    parts = over_sections(jnp.where(first, q, o), jnp.where(first, o, q))
    return grad_hidden + more, parts


def on_device(
    inputs, cotangent, segments, routes, route_gates, attn_gain, w_query, key_weight,
    value_weight, w_out, mixer_gain, w_gate, w_up, w_down,
):
    section = lax.axis_index(S)
    first = section == 0
    at = lax.axis_index(T)
    rows, width = inputs.shape[1:]
    length = segments.shape[2]
    here = w_gate.shape[1]
    hidden = w_gate.shape[3]
    experts = lax.axis_size(D) * here
    mine = lambda a: lax.dynamic_index_in_dim(a, section, 0, False)
    theirs = lambda a: lax.dynamic_index_in_dim(a, 1 - section, 0, False)
    x0 = mine(inputs)
    grad1 = mine(cotangent)
    segment = mine(segments)[0]

    def halves(own):
        keep, got = mine(own), partner(theirs(own))
        return jnp.where(first, keep, got), jnp.where(first, got, keep)

    named = routes[0][..., None] == jnp.arange(experts, dtype=jnp.int32)
    shares = jnp.sum(jnp.where(named, route_gates[0][..., None], 0.0), 2)
    shares = jnp.stack(halves(shares), 1)

    shares = line_gather(shares)

    def factors(own, l):
        share = own[:, l]
        share = lax.dynamic_slice_in_dim(share, lax.axis_index(D) * here, here, 1)
        share = jnp.stack([jnp.where(first, share[:, i], share[:, 1 - i]) for i in range(2)], 1)
        return jnp.broadcast_to(share.T.reshape(here, -1, rows, 1), (here, share.shape[0] // rows, rows, HEAD)), share

    queries_at = at * rows + jnp.arange(rows)
    keys_at = jnp.concatenate([(at ^ r) * rows + jnp.arange(rows) for r in range(4)])
    key_segment = jnp.concatenate([lax.dynamic_slice_in_dim(segment, (at ^ r) * rows, rows, 0) for r in range(4)])
    allowed = (keys_at[None] <= queries_at[:, None]) & (key_segment[:rows, None] == key_segment[None])
    c = dict(rope=rope_tables(queries_at.astype(F32)), bias=jnp.where(allowed, 0.0, -1e30))

    attn = halves(jnp.stack([w_query[0].T, w_out[0]]))
    g, u = (w[0].transpose(0, 2, 1) for w in (w_gate, w_up))
    ffn = halves(jnp.stack([g, u, w_down[0]], 1))
    kv = both(first, jnp.concatenate([key_weight[0], value_weight[0]], 1))
    ga = both(first, attn_gain)
    gm = both(first, mixer_gain)
    n = lax.axis_size(D)
    small = [dict(kv=kv[l], ga=ga[l], gm=gm[l], unit=hidden) for l in range(2)]
    for l, one in enumerate(small):
        one["wide"], one["share"] = factors(shares, l)
    grads = along(low(grad1)) if n <= SMALL else low(grad1)
    ffn = [v.reshape(-1, width) for v in ffn]
    high = w_out.shape[1]

    ahead = keys_and_values(x0, small[0], c)
    got = pieces_of(attn[0])
    late = after(ffn[0], got, ahead, grads, shares)
    mine = jnp.concatenate(got)
    small[0].update(mine=mine, other=partner(mine))
    hidden0, mixer, k0 = attention_forward(x0, *ahead, small[0], c)
    got = pieces_of(late)
    crossed = after(got, mixer)
    small[0].update(pieces=got + [partner(v) for v in crossed])
    more = pieces_of(after(jnp.concatenate([attn[1], ffn[1]]), got))
    y, kept = mix_forward(mixer, small[0], n)
    y0 = low((hidden0 + y))
    other = [partner(v) for v in after(more, y)]
    small[1].update(
        mine=jnp.concatenate([v[:high] for v in more]), other=jnp.concatenate([v[:high] for v in other]),
        pieces=more + other,
    )
    hidden1, mixer, k1 = attention_forward(y0, *keys_and_values(y0, small[1], c, other), small[1], c)
    y, gm, keep, give = mix_both(mixer, low(grad1), small[1], n, grads)
    parts = over_sections(keep, give)
    gx1, more = attention_backward(grad1, gm, k1, small[1], c, first)
    gb = low(gx1)
    rows_f = 3 * hidden
    both_parts = [jnp.concatenate([a.reshape(rows_f, width), b]) for a, b in zip(parts, more)]
    gb, both_parts = lax.optimization_barrier((gb, both_parts))
    got = summed(both_parts)
    gm, keep, give = mix_backward(gb, kept, small[0], n)
    gm, got, y = lax.optimization_barrier((gm, got, y))
    y1 = low(hidden1 + (scatter_along(y).astype(F32) if n <= SMALL else y))
    f1, s1 = got[:rows_f].reshape(3, hidden, width), lax.psum(got[rows_f:], D)
    parts = over_sections(keep, give)
    gx0, more = attention_backward(gb.astype(F32), gm, k0, small[0], c, first)
    s0 = summed(more)
    f0 = summed(after(parts, s0))
    s0 = lax.psum(after(s0, s1, y1), D)

    outs = jnp.stack(swap(first, y0, y1))
    input_grads = jnp.stack(swap(first, low(gx0), low(gx1))).astype(F32)
    f = jnp.stack(swap(first, f0, f1)).astype(F32)
    zero, one = swap(first, s0, s1)
    q, o = zero[:high].astype(F32), one[:high].astype(F32)
    less = jnp.stack(pieces_of(jnp.stack([zero[high:], one[high:]])))
    less = jnp.concatenate([lax.dynamic_index_in_dim(less, at ^ i, 0, False) for i in range(4)], 1).astype(F32)
    ka, vm = less[0], less[1]
    few = GROUPS * HEAD
    return (
        outs[None], input_grads[None], ka[few : few + 1], q.T[None], ka[:few].T[None],
        vm[:few].T[None], o[None], vm[few : few + 1], f[:, 0].transpose(0, 2, 1)[None],
        f[:, 1].transpose(0, 2, 1)[None], f[:, 2][None],
    )


def solution(mesh):
    rows, layer, cols = P(None, (D, T), None), P(S, None, (D, T), None), P(S, D, None, T)
    in_specs = (
        rows, rows, P(None, D, None), layer, layer, P(S, None), P(S, None, T), P(S, None, None),
        P(S, None, None), P(S, T, None), P(S, None), cols, cols, P(S, D, T, None),
    )
    out_specs = (
        layer, layer, P(S, None), P(S, None, T), P(S, None, None), P(S, None, None), P(S, T, None),
        P(S, None), cols, cols, P(S, D, T, None),
    )
    return jax.shard_map(on_device, mesh=mesh, in_specs=in_specs, out_specs=out_specs, check_vma=False)
```
